32 devices in a mesh: rep: 4 (over x, core), shard: 8 (over z, y).
Axes of the slice: x: 2, y: 2, z: 4, core: 2. Of those that a mesh axis runs over, the one named last changes fastest.
Arguments:
- stream: float32 [8192, 768], P(('rep', 'shard')), may hold values from -6 to 6
- prev_logits: float32 [8192, 8], P(('rep', 'shard')), may hold values from -3 to 3
- segments: int32 [32, 256], P(('rep', 'shard')), may hold values from 0 to 3, never falling along the last dimension, each value on 1 to 128 neighbouring positions
- routes: int32 [8192, 2], P(('rep', 'shard')), may hold values from 0 to 7, all different within a row
- claim_order: int32 [32, 256], P(('rep', 'shard')), may hold values from 0 to 255, each once within a row
- out_cotangent: float32 [8192, 768], P(('rep', 'shard')), may hold values from -6 to 6
- first_gain: bfloat16 [768], P('shard'), may hold values from 0.5 to 1.5
- attend_weight: bfloat16 [768, 2304], P('shard'), may hold values from -0.21875 to 0.21875
- output_weight: bfloat16 [768, 768], P('shard'), may hold values from -0.625 to 0.625
- second_gain: bfloat16 [768], P('shard'), may hold values from 0.5 to 1.5
- router_weight: bfloat16 [768, 8], P('shard'), may hold values from -0.15625 to 0.15625
- constant_mix: bfloat16 [768, 4], P('shard'), may hold values from -0.21875 to 0.21875
- constant_vector: bfloat16 [768, 2], P('shard'), may hold values from -6 to 6
- expert_in: bfloat16 [768, 4, 4096], P('shard'), may hold values from -0.21875 to 0.21875
- expert_out: bfloat16 [2048, 4, 768], P('shard'), may hold values from -1 to 1
Outputs:
- result: bfloat16 [8192, 768], P(('rep', 'shard'))
- stream_grad: float32 [8192, 768], P(('rep', 'shard'))
- logits_grad: float32 [8192, 8], P(('rep', 'shard'))
- first_gain_grad: float32 [768], P('shard')
- attend_grad: float32 [768, 2304], P('shard')
- output_grad: float32 [768, 768], P('shard')
- second_gain_grad: float32 [768], P('shard')
- router_grad: float32 [768, 8], P('shard')
- mix_grad: float32 [768, 4], P('shard')
- vector_grad: float32 [768, 2], P('shard')
- expert_in_grad: float32 [768, 4, 4096], P('shard')
- expert_out_grad: float32 [2048, 4, 768], P('shard')
The draws below stay inside these ranges and needn't reach their ends.
Inputs may be any that keep to these rules, and one draw needn't show every extreme that they name: `segments`: within a row segment numbers never fall. `routes`: the 2 experts of a token differ. `claim_order`: each row holds every number below 256 once.
All inputs are finite; a program needn't handle non-finite values.
Results may differ from the reference program's by a relative error of at most 0.017.
Values may be sent and summed in bfloat16 or wider, within the bound.
No kernel may reach another device: no remote copies, remote signals or barrier semaphores. Data moves between devices by JAX's collectives and lax.ppermute only.
A program may use at most 320 MiB of HBM per device.

```python
import math
import jax
import jax.numpy as jnp
import numpy as np
from jax import lax

D = 768
H = 12
HD = 64
FF = 2048
E_FFN = 4
NC = 2
TOP = 2
NE = 8
TOK_DEV = 256
CAP = 64
ROWS = 32
TOKENS = 8192


def levels(rng, shape, pieces, low, high):
    loudness, own = 1.0, jax.random.fold_in(rng, 6)
    for dim, blocks in pieces:
        steps = jnp.exp(jax.random.uniform(jax.random.fold_in(own, dim), (blocks,), jnp.float32, low / len(pieces), high / len(pieces)))
        loudness = loudness * jnp.repeat(steps, shape[dim] // blocks).reshape([-1 if axis == dim else 1 for axis in range(len(shape))])
    return loudness


def choose_distinct(rng, rows, count, top, lift):
    order = jax.random.permutation(jax.random.fold_in(rng, 1), count)
    boost = order
    for power in range(3):
        boost = boost * boost // count
    boost = boost * lift // count
    lots = jax.random.randint(jax.random.fold_in(rng, 2), (rows, count), 0, 4096) + boost
    sure = jax.random.permutation(jax.random.fold_in(rng, 3), rows)[jnp.arange(count) % rows]
    lots = jnp.where(jnp.arange(rows)[:, None] == sure[None, :], 1 << 14, lots)
    priority = lots * count + jnp.arange(count)
    return lax.top_k(priority.astype(jnp.int32), top)[1].astype(jnp.int32)


def profile(number_of, total, limit, skew):
    loads = [(1 << 20) // math.isqrt(standing ** skew) + 1 for standing in range(2, number_of + 1)]
    surplus, holding = total - limit - (number_of - 1), [1] * (number_of - 1)
    while surplus > 0:
        movable = [i for i in range(number_of - 1) if holding[i] < limit]
        mass, budget = sum([loads[i] for i in movable]), surplus
        for i in movable:
            extra = min(limit - holding[i], max(1, budget * loads[i] // mass), surplus)
            holding[i] = holding[i] + extra
            surplus = surplus - extra
    return np.array([limit] + holding)


def uneven(rng, number_of, total, reach, skew):
    if number_of == 2:
        one = jax.random.randint(rng, (), max(1, total - reach), min(reach, total - 1) + 1)
        return jnp.stack([one, total - one])
    lengths = jnp.asarray(profile(number_of, total, reach, skew), jnp.int32)
    couples = (number_of - 1) // 2
    source_of, taker = lengths[1:1 + 2 * couples:2], lengths[2:2 + 2 * couples:2]
    room = jnp.minimum(source_of - 1, reach - taker)
    moved = jax.random.randint(jax.random.fold_in(rng, 1), (couples,), 0, 1 << 20) % (room + 1)
    lengths = lengths.at[1:1 + 2 * couples:2].set(source_of - moved).at[2:2 + 2 * couples:2].set(taker + moved)
    return lengths[jax.random.permutation(jax.random.fold_in(rng, 2), number_of)]


def noise(own_key, extent, spread, limit, pieces=(), held_as=jnp.bfloat16):
    level = levels(own_key, extent, pieces, -0.22, 0.18) if pieces else 1.0
    entries = jax.random.normal(own_key, extent, jnp.float32) * spread * level
    return jnp.minimum(jnp.maximum(entries, -limit), limit).astype(held_as)


def setup_inputs(seed: int = 0) -> dict:
    keys = jax.random.split(jax.random.key(seed), 16)
    stream = noise(keys[0], (TOKENS, D), 1.0, 6.0, ((0, 32),), jnp.float32)
    prev_logits = noise(keys[1], (TOKENS, NE), 0.5, 3.0, ((0, 32),), jnp.float32)
    segments = jax.vmap(lambda own: jnp.searchsorted(jnp.cumsum(uneven(own, 4, TOK_DEV, TOK_DEV // 2, 2)), jnp.arange(TOK_DEV), side="right"))(jax.random.split(keys[2], ROWS)).reshape((ROWS, TOK_DEV)).astype(jnp.int32)
    routes = choose_distinct(keys[3], TOKENS, NE, TOP, 2048)
    claim_order = jax.vmap(lambda own: jax.random.permutation(own, TOK_DEV))(jax.random.split(keys[4], ROWS)).reshape((ROWS, TOK_DEV)).astype(jnp.int32)
    out_cotangent = noise(keys[5], (TOKENS, D), 1.0, 6.0, ((0, 32),), jnp.float32)
    first_gain = jnp.clip(1.0 + 0.1 * jax.random.normal(keys[6], (D,), jnp.float32), 0.5, 1.5).astype(jnp.bfloat16)
    attend_weight = noise(keys[7], (D, 3 * D), D ** -0.5, 0.21875, ((0, 8),))
    output_weight = noise(keys[8], (D, D), (D // 8) ** -0.5, 0.625, ((0, 8),))
    second_gain = jnp.clip(1.0 + 0.1 * jax.random.normal(keys[9], (D,), jnp.float32), 0.5, 1.5).astype(jnp.bfloat16)
    router_weight = noise(keys[10], (D, NE), (2 * D) ** -0.5, 0.15625, ((0, 8),))
    constant_mix = noise(keys[11], (D, 2 * NC), D ** -0.5, 0.21875, ((0, 8),))
    constant_vector = noise(keys[12], (D, NC), 1.0, 6.0, ((0, 8),))
    expert_in = noise(keys[13], (D, E_FFN, 2 * FF), D ** -0.5, 0.21875, ((0, 8),))
    expert_out = noise(keys[14], (FF, E_FFN, D), (FF // 64) ** -0.5, 1.0, ((0, 8),))
    return {"stream": stream, "prev_logits": prev_logits, "segments": segments, "routes": routes, "claim_order": claim_order, "out_cotangent": out_cotangent, "first_gain": first_gain, "attend_weight": attend_weight, "output_weight": output_weight, "second_gain": second_gain, "router_weight": router_weight, "constant_mix": constant_mix, "constant_vector": constant_vector, "expert_in": expert_in, "expert_out": expert_out}


EPSILON = 1e-06
HIGHEST = lax.Precision.HIGHEST

@jax.custom_vjp
def low(v):
    return lax.optimization_barrier(v.astype(jnp.bfloat16)).astype(jnp.float32)

@jax.custom_vjp
def low_back(v):
    return v

def low_keep(v):
    return (low(v), None)

def low_pass(kept, grad):
    return (grad,)

def back_keep(v):
    return (v, None)

def back_low(kept, grad):
    return (low(grad),)
low.defvjp(low_keep, low_pass)
low_back.defvjp(back_keep, back_low)

def rotary_tables(length, head_size):
    half = head_size // 2
    position = jnp.arange(length, dtype=jnp.float32)
    frequency = jnp.exp(jnp.arange(half, dtype=jnp.float32) * (-2.0 * math.log(10000.0) / head_size))
    angle = position[:, None] * frequency[None, :]
    return (jnp.cos(angle), jnp.sin(angle))

def rotate(values, cosine, sine):
    half = values.shape[-1] // 2
    first = values[..., :half]
    second = values[..., half:]
    cosine = cosine[:, None, :]
    sine = sine[:, None, :]
    return jnp.concatenate([first * cosine - second * sine, second * cosine + first * sine], axis=-1)

def assign_slots(route_row, order_row, experts, capacity):
    tokens = route_row.shape[0]
    top = route_row.shape[1]
    claims = jnp.take(route_row, order_row, axis=0).reshape(-1).astype(jnp.int32)
    onehot = (claims[:, None] == jnp.arange(experts, dtype=jnp.int32)[None, :]).astype(jnp.int32)
    before = (jnp.cumsum(onehot, axis=0, dtype=jnp.int32) - onehot).astype(jnp.int32)
    place = lax.optimization_barrier(jnp.sum(before * onehot, axis=1, dtype=jnp.int32)).astype(jnp.int32)
    kept = (claims < experts) & (place < capacity)
    target = jnp.where(kept, claims * capacity + place, experts * capacity).astype(jnp.int32)
    owner = jnp.repeat(order_row, top).astype(jnp.int32)
    by_token = jnp.zeros((tokens, top), jnp.int32).at[order_row].set(target.reshape(tokens, top))
    table = jnp.full((experts * capacity + 1,), tokens, jnp.int32).at[target].set(owner)[:experts * capacity]
    return (by_token, table)

def row_forward(stream, prev_logits, segment_row, route_row, order_row, first_gain, attend_weight, output_weight, second_gain, router_weight, constant_mix, constant_vector, expert_in, expert_out):
    tokens, width = stream.shape
    scale = 1.0 / math.sqrt(HD)
    inverse_one = lax.rsqrt(lax.optimization_barrier(jnp.mean(stream * stream, axis=-1, keepdims=True)) + EPSILON)
    normed = low(stream * inverse_one * first_gain)
    projected = low_back(jnp.dot(normed, attend_weight, precision=HIGHEST)).reshape(tokens, 3, H, HD)
    cosine, sine = rotary_tables(tokens, HD)
    queries = low(rotate(projected[:, 0], cosine, sine))
    key_rows = low(rotate(projected[:, 1], cosine, sine))
    value_rows = low(projected[:, 2])
    scores = low_back(scale * jnp.einsum('qhd,khd->hqk', queries, key_rows, precision=HIGHEST))
    position = jnp.arange(tokens)
    allowed = (segment_row[:, None] == segment_row[None, :]) & (position[None, :] <= position[:, None])
    probs = low(jax.nn.softmax(jnp.where(allowed[None], scores, -1e+30), axis=-1))
    mixed = jnp.einsum('hqk,khd->qhd', probs, value_rows, precision=HIGHEST).reshape(tokens, width)
    mixed = low_back(low(mixed))
    hidden = stream + low_back(jnp.dot(mixed, output_weight, precision=HIGHEST))
    inverse_two = lax.rsqrt(lax.optimization_barrier(jnp.mean(hidden * hidden, axis=-1, keepdims=True)) + EPSILON)
    routed_in = low(hidden * inverse_two * second_gain)
    logits = jnp.dot(routed_in, router_weight, precision=HIGHEST) + prev_logits
    chances = jax.nn.softmax(logits, axis=-1)
    gates = jnp.take_along_axis(chances, route_row, axis=1)
    onehot = (route_row[:, :, None] == jnp.arange(NE, dtype=jnp.int32)[None, None, :]).astype(jnp.float32)
    combine = lax.optimization_barrier(jnp.sum(gates[:, :, None] * onehot, axis=1))
    by_token, table = assign_slots(route_row, order_row, E_FFN, CAP)
    padded = jnp.concatenate([routed_in, jnp.zeros((1, width), jnp.float32)], axis=0)
    slot_in = jnp.take(padded, table, axis=0).reshape(E_FFN, CAP, width)
    gate_up = low_back(jnp.einsum('ecd,def->ecf', slot_in, expert_in, precision=HIGHEST))
    activated = low(jax.nn.silu(gate_up[..., :FF]) * gate_up[..., FF:])
    slot_out = low_back(jnp.einsum('ecf,fej->ecj', activated, expert_out, precision=HIGHEST)).reshape(E_FFN * CAP, width)
    padded_out = jnp.concatenate([slot_out, jnp.zeros((1, width), jnp.float32)], axis=0)
    picked = jnp.take(padded_out, by_token, axis=0)
    expert_sum = lax.optimization_barrier(jnp.sum(gates[:, :, None] * picked, axis=1))
    copy_term = combine[:, E_FFN + 1:E_FFN + 2] * routed_in
    mixing = jax.nn.softmax(jnp.dot(routed_in, constant_mix, precision=HIGHEST).reshape(tokens, NC, 2), axis=-1)
    constant_out = mixing[..., 0:1] * routed_in[:, None, :] + mixing[..., 1:2] * constant_vector.T[None]
    constant_term = lax.optimization_barrier(jnp.sum(combine[:, E_FFN + 2:, None] * constant_out, axis=1))
    return hidden + expert_sum + copy_term + constant_term

def reference(stream, prev_logits, segments, routes, claim_order, out_cotangent, first_gain, attend_weight, output_weight, second_gain, router_weight, constant_mix, constant_vector, expert_in, expert_out):
    rows, length = segments.shape
    width = stream.shape[1]
    group = min(rows, max(1, 4096 // length))
    blocks = rows // group

    def group_forward(stream_b, prev_b, segment_b, route_b, order_b, weight_list):
        return jax.vmap(row_forward, in_axes=(0, 0, 0, 0, 0) + (None,) * 9)(stream_b, prev_b, segment_b, route_b, order_b, *weight_list)
    saved = jax.checkpoint(group_forward)

    def whole(stream_f, prev_f, *weights):

        def step(carry, block):
            return (carry, saved(block[0], block[1], block[2], block[3], block[4], weights))
        inputs = (stream_f.reshape(blocks, group, length, width), prev_f.reshape(blocks, group, length, NE), segments.reshape(blocks, group, length), routes.reshape(blocks, group, length, TOP), claim_order.reshape(blocks, group, length))
        unused, outputs = lax.scan(step, jnp.zeros((), jnp.float32), inputs)
        return outputs.reshape(rows * length, width)
    floats = [array.astype(jnp.float32) for array in (first_gain, attend_weight, output_weight, second_gain, router_weight, constant_mix, constant_vector, expert_in, expert_out)]
    result, pullback = jax.vjp(whole, stream.astype(jnp.float32), prev_logits.astype(jnp.float32), *floats)
    grads = pullback(out_cotangent.astype(jnp.float32))
    return (result.astype(jnp.bfloat16), grads[0], grads[1], grads[2], grads[3], grads[4], grads[5], grads[6], grads[7], grads[8], grads[9], grads[10])
```

```python
import math

import jax
import jax.numpy as jnp
import numpy as np
from jax import lax
from jax.experimental import pallas as pl
from jax.experimental.pallas import tpu as pltpu
from jax.sharding import PartitionSpec as P

H = 12
HD = 64
FF = 2048
E_FFN = 4
NC = 2
NE = 8
CAP = 64
D = 768
T = 256
GROUP = 8
ROWS = D // GROUP
HALF = ROWS // 2
WIDE = 2 * D
QUARTER = FF // 4

EPSILON = 1e-06
BF = jnp.bfloat16
F32 = jnp.float32
I32 = jnp.int32
AXES = ("rep", "shard")
VMEM_LIMIT = 56 << 20


def nn(a, b):
    return lax.dot_general(a, b, (((1,), (0,)), ((), ())), preferred_element_type=F32)


def nt(a, b):
    return lax.dot_general(a, b, (((1,), (1,)), ((), ())), preferred_element_type=F32)


def tn(a, b):
    return lax.dot_general(a, b, (((0,), (0,)), ((), ())), preferred_element_type=F32)


def exact(a, b, dims):
    return lax.dot_general(
        a, b, (dims, ((), ())), precision=lax.Precision.HIGHEST, preferred_element_type=F32
    )


def iota(shape, dim):
    return lax.broadcasted_iota(I32, shape, dim)


def split(v):
    high = v.astype(BF)
    return high, (v - high.astype(F32)).astype(BF)


def tables():
    half = HD // 2
    position = np.arange(T, dtype=np.float32)
    frequency = np.exp(
        np.arange(half, dtype=np.float32) * np.float32(-2.0 * math.log(10000.0) / HD)
    ).astype(np.float32)
    angle = (position[:, None] * frequency[None, :]).astype(np.float32)
    cosine, sine = np.cos(angle), np.sin(angle)
    return (
        np.concatenate([cosine] * 4, axis=1).astype(np.float32),
        np.concatenate([-sine, sine] * 2, axis=1).astype(np.float32),
    )


def swapped(tile):
    lane = iota(tile.shape, 1) % HD
    return jnp.where(lane < HD // 2, pltpu.roll(tile, 96, 1), pltpu.roll(tile, 32, 1))


def call(body, out_shape, in_specs, scratch=(), flops=0, moved=0):
    return pl.pallas_call(
        body,
        out_shape=out_shape,
        in_specs=in_specs,
        out_specs=jax.tree.map(lambda _: pl.BlockSpec(memory_space=pltpu.VMEM), out_shape),
        scratch_shapes=list(scratch),
        compiler_params=pltpu.CompilerParams(vmem_limit_bytes=VMEM_LIMIT),
        cost_estimate=pl.CostEstimate(flops=flops, bytes_accessed=moved, transcendentals=0),
    )


SMEM = pl.BlockSpec(memory_space=pltpu.SMEM)
VM = pl.BlockSpec(memory_space=pltpu.VMEM)
ANY = pl.BlockSpec(memory_space=pl.ANY)


def shape(*dims, dtype=BF):
    return jax.ShapeDtypeStruct(dims, dtype)


def start_weights(pos, pieces, target, sems):
    x, c, z, y = (pos[i] for i in range(4))
    copies = []
    for p in range(4):
        column = pl.multiple_of((x ^ (p >> 1)) * WIDE, 128)
        for cr in range(2):
            for kz in range(4):
                row = ((z ^ kz) * 2 + (y ^ (p & 1))) * ROWS + (c ^ cr) * HALF
                copies.append(
                    pltpu.make_async_copy(
                        pieces[2 * p + cr].at[pl.ds(kz * HALF, HALF), :],
                        target.at[pl.ds(pl.multiple_of(row, 16), HALF), pl.ds(column, WIDE)],
                        sems.at[len(copies)],
                    )
                )
    for copy in copies:
        copy.start()
    return copies


def route_body(pos, routes, order, grad, prev, g0, g1, g2, g3, disp_out):
    here = 2 * pos[0] + pos[3]
    row, col = iota((T, T), 0), iota((T, T), 1)
    lane = iota((T, 16), 1)
    claims = jnp.where(order[...] == row, 1.0, 0.0).astype(BF)
    r = routes[...]
    chosen = ((r[:, 0:1] == lane) | (r[:, 1:2] == lane)) & (lane < E_FFN)
    ranked = tn(claims, jnp.where(chosen, 1.0, 0.0).astype(BF))
    before = nn(jnp.where(col < row, 1.0, 0.0).astype(BF), ranked.astype(BF))
    place = nn(claims, before.astype(BF))
    kept = chosen & (place < CAP)
    dispatch = jnp.zeros((T, T), F32)
    colf = col.astype(F32)
    for p in range(4):
        mine = kept & (lane == (here ^ p))
        target = jnp.sum(jnp.where(mine, place + (p * CAP + 1.0), 0.0), axis=1, keepdims=True)
        dispatch = dispatch + jnp.where(colf == target - 1.0, 1.0, 0.0)
    dispatch = dispatch.astype(BF)
    disp_out[...] = dispatch
    slots = tn(dispatch, grad[...].astype(BF)).astype(BF)
    extra = tn(dispatch, prev[...]).astype(BF)
    for p, out in enumerate((g0, g1, g2, g3)):
        out[:, :D] = slots[p * CAP : (p + 1) * CAP]
        out[:, D:] = extra[p * CAP : (p + 1) * CAP]


def attend_body(
    pos, stream, small, seg, cos, sin, disp, w0, w1, w2, w3, w4, w5, w6, w7,
    normed_out, q_out, k_out, v_out, probs_out, mixed_out, hidden_out, routed_out,
    x0, x1, x2, x3, weights, sems,
):
    copies = start_weights(pos, (w0, w1, w2, w3, w4, w5, w6, w7), weights, sems)
    s = stream[...]
    r1 = lax.rsqrt(jnp.mean(s * s, axis=1, keepdims=True) + EPSILON)
    normed = (s * r1 * small[14:15, :].astype(F32)).astype(BF)
    normed_out[...] = normed
    row, col = iota((T, T), 0), iota((T, T), 1)
    segf = seg[...].astype(F32)
    segcol = jnp.sum(jnp.where(row == col, segf, 0.0), axis=1, keepdims=True)
    allowed = (segcol == segf) & (col <= row)
    cosine, sine = cos[...], sin[...]
    for copy in copies:
        copy.wait()
    for n in range(9):
        part = nn(normed, weights[:, n * 256 : (n + 1) * 256])
        out, base = (q_out, k_out, v_out)[n // 3], (n % 3) * 256
        for t in range(2):
            tile = part[:, t * 128 : (t + 1) * 128]
            if n < 6:
                tile = tile * cosine + swapped(tile) * sine
            out[:, base + t * 128 : base + (t + 1) * 128] = tile.astype(BF)
    first = iota((T, 128), 1) < HD
    for j in range(H // 2):
        cols = slice(j * 128, (j + 1) * 128)
        q2, k2, v2 = q_out[:, cols], k_out[:, cols], v_out[:, cols]
        halves = []
        for hh in range(2):
            mask = first if hh == 0 else ~first
            qm = jnp.where(mask, q2.astype(F32), 0.0).astype(BF)
            scores = jnp.where(allowed, nt(qm, k2) * (1.0 / math.sqrt(HD)), -1e30)
            raised = jnp.exp(scores - jnp.max(scores, axis=1, keepdims=True))
            probs = (raised / jnp.sum(raised, axis=1, keepdims=True)).astype(BF)
            probs_out[2 * j + hh] = probs
            halves.append(nn(probs, v2))
        mixed_out[:, cols] = jnp.where(first, halves[0], halves[1]).astype(BF)
    hidden = s + nn(mixed_out[...], weights[:, 3 * D :])
    hidden_out[...] = hidden
    r2 = lax.rsqrt(jnp.mean(hidden * hidden, axis=1, keepdims=True) + EPSILON)
    routed = (hidden * r2 * small[15:16, :].astype(F32)).astype(BF)
    routed_out[...] = routed
    slots = tn(disp[...], routed).astype(BF)
    for p, out in enumerate((x0, x1, x2, x3)):
        out[...] = slots[p * CAP : (p + 1) * CAP]


def column(v, lane, index):
    return jnp.sum(jnp.where(lane == index, v, 0.0), axis=1, keepdims=True)


def chance(logits, lane):
    masked = jnp.where(lane < NE, logits, -1e30)
    raised = jnp.where(lane < NE, jnp.exp(masked - jnp.max(masked, axis=1, keepdims=True)), 0.0)
    return raised / jnp.sum(raised, axis=1, keepdims=True)


def router_body(hidden, routed, small, prev, routes, grad, base_out, aux_out):
    lane = iota((T, 16), 1)
    rin = routed[...].astype(F32)
    g = grad[...]
    logits = nt(routed[...], small[...])
    chances = chance(logits + prev[...], lane)
    r = routes[...]
    chosen = (r[:, 0:1] == lane) | (r[:, 1:2] == lane)
    combine = jnp.where(chosen, chances, 0.0)
    copy_weight = column(combine, lane, E_FFN + 1)
    copy_grad = jnp.sum(g * rin, axis=1, keepdims=True)
    base = hidden[...] + copy_weight * rin
    others = jnp.where(lane == E_FFN + 1, copy_grad, 0.0)
    mixing_grad = jnp.zeros((T, 16), F32)
    factor = copy_weight
    for n in range(NC):
        l0, l1 = column(logits, lane, 8 + 2 * n), column(logits, lane, 9 + 2 * n)
        a0, a1 = 1.0 / (1.0 + jnp.exp(l1 - l0)), 1.0 / (1.0 + jnp.exp(l0 - l1))
        vector = small[12 + n : 13 + n, :].astype(F32)
        weight = column(combine, lane, E_FFN + 2 + n)
        base = base + weight * (a0 * rin + a1 * vector)
        vector_dot = jnp.sum(g * vector, axis=1, keepdims=True)
        others = others + jnp.where(
            lane == E_FFN + 2 + n, a0 * copy_grad + a1 * vector_dot, 0.0
        )
        d0, d1 = weight * copy_grad, weight * vector_dot
        total = a0 * d0 + a1 * d1
        mixing_grad = mixing_grad + jnp.where(lane == 8 + 2 * n, a0 * (d0 - total), 0.0)
        mixing_grad = mixing_grad + jnp.where(lane == 9 + 2 * n, a1 * (d1 - total), 0.0)
        mixing_grad = mixing_grad + jnp.where(lane == 12 + n, a1 * weight, 0.0)
        factor = factor + a0 * weight
    base_out[...] = base
    aux_out[:, 0:16] = chances
    aux_out[:, 16:32] = combine
    aux_out[:, 32:48] = jnp.where(chosen, others, 0.0)
    aux_out[:, 48:64] = mixing_grad
    aux_out[:, 64:128] = jnp.broadcast_to(factor, (T, 64))


def expert_body(
    pos, x0, x1, x2, x3, g0, g1, g2, g3, v0, v1, v2, v3, e0, e1, e2, e3,
    send_out, keep_out, act_out, grad_out, win_out, wout_out,
):
    z, y = pos[2], pos[3]
    for kz, piece in enumerate((v0, v1, v2, v3)):
        for yr in range(2):
            row = pl.multiple_of(((z ^ kz) * 2 + (y ^ yr)) * ROWS, 16)
            win_out[pl.ds(row, ROWS), :] = piece[yr * ROWS : (yr + 1) * ROWS, :]
    wout_out[:256] = e0[...] + e1[...]
    wout_out[256:] = e2[...] + e3[...]
    win, wout = win_out[...], wout_out[...]
    ones = jnp.ones((16, QUARTER), F32)
    for b, (xs, gs) in enumerate(((x0, g0), (x1, g1), (x2, g2), (x3, g3))):
        rows = slice(b * 256, (b + 1) * 256)
        gate_up = nn(xs[...], win)
        a, u = gate_up[:, :QUARTER], gate_up[:, QUARTER:]
        sigma = 1.0 / (1.0 + jnp.exp(-a))
        swish = a * sigma
        activated = (swish * u).astype(BF)
        act_out[rows, :] = activated
        back = nt(gs[:, :D], wout)
        dots = exact(ones, activated.astype(F32) * back, ((1,), (1,)))[0:1]
        gate_grad = back * u * sigma * (1.0 + a * (1.0 - sigma))
        both = jnp.concatenate([gate_grad.astype(BF), (back * swish).astype(BF)], axis=1)
        grad_out[rows, :] = both
        slot_grad = nt(both, win)
        at = (b % 2) * 272
        if b < 2:
            keep_out[at : at + 256, :] = slot_grad
            keep_out[at + 256 : at + 272, :] = jnp.zeros((16, D), F32)
            keep_out[at + 256 : at + 257, 0:256] = dots
        else:
            high, low = split(dots)
            send_out[at : at + 256, :] = slot_grad.astype(BF)
            send_out[at + 256 : at + 272, :] = jnp.zeros((16, D), BF)
            send_out[at + 256 : at + 258, 0:256] = jnp.concatenate([high, low], axis=0)


def fold_body(keep, got, send_out, keep_out):
    total = keep[...] + got[...].astype(F32)
    dots = [keep[n * 272 + 256 : n * 272 + 257, 0:256]
            + got[n * 272 + 256 : n * 272 + 257, 0:256].astype(F32)
            + got[n * 272 + 257 : n * 272 + 258, 0:256].astype(F32) for n in range(2)]
    keep_out[0:256, :] = total[0:256]
    keep_out[256:272, :] = jnp.zeros((16, D), F32)
    keep_out[256:257, 0:256] = dots[0]
    high, low = split(dots[1])
    send_out[0:256, :] = total[272:528].astype(BF)
    send_out[256:272, :] = jnp.zeros((16, D), BF)
    send_out[256:258, 0:256] = jnp.concatenate([high, low], axis=0)


def spread_body(keep, got, r0, r1, r2, r3):
    total = (keep[0:256, :] + got[0:256, :].astype(F32)).astype(BF)
    dots = (
        keep[256:257, 0:256] + got[256:257, 0:256].astype(F32) + got[257:258, 0:256].astype(F32)
    )
    high, low = split(dots)
    for p, out in enumerate((r0, r1, r2, r3)):
        out[0:CAP, :] = total[p * CAP : (p + 1) * CAP]
        out[CAP : CAP + 16, :] = jnp.zeros((16, D), BF)
        out[CAP : CAP + 2, 0:256] = jnp.concatenate([high, low], axis=0)


def slots_out_body(act, wout, send_out, keep_out):
    for b in range(4):
        part = nn(act[b * 256 : (b + 1) * 256, :], wout[...]).astype(BF)
        out = (keep_out, send_out)[b // 2]
        out[(b % 2) * 256 : (b % 2 + 1) * 256, :] = part


def weight_grad_body(
    pos, x0, x1, x2, x3, g0, g1, g2, g3, act, grad, small,
    d0, d1, d2, d3, o0, o1, scaled, whole,
):
    x, z, y = pos[0], pos[2], pos[3]
    lane = iota((256, 16), 1)
    expert = 2 * x + y
    total = jnp.zeros((QUARTER, D), F32)
    xs = jnp.concatenate([v[...] for v in (x0, x1, x2, x3)], axis=0)
    for b, (xv, gs) in enumerate(((x0, g0), (x1, g1), (x2, g2), (x3, g3))):
        rows = slice(b * 256, (b + 1) * 256)
        prev = gs[:, D : D + 16].astype(F32) + gs[:, D + 16 : D + 32].astype(F32)
        chances = chance(nt(xv[...], small[...]) + jnp.where(lane < NE, prev, 0.0), lane)
        weight = column(chances, lane, expert)
        scaled[rows, :] = (grad[rows, :].astype(F32) * weight).astype(BF)
        total = total + tn(act[rows, :], (gs[:, :D].astype(F32) * weight).astype(BF))
    o0[...] = total[:256].astype(BF)
    o1[...] = total[256:].astype(BF)
    for n in range(4):
        cols = slice(n * 256, (n + 1) * 256)
        whole[:, cols] = tn(xs, scaled[:, cols]).astype(BF)
    for kz, out in enumerate((d0, d1, d2, d3)):
        for yr in range(2):
            row = pl.multiple_of(((z ^ kz) * 2 + (y ^ yr)) * ROWS, 16)
            out[yr * ROWS : (yr + 1) * ROWS, :] = whole[pl.ds(row, ROWS), :]


def back_body(
    pos, r0, r1, r2, r3, disp, hidden_in, routed, aux, grad, small, stream, normed, q, k, v,
    probs, mixed, cos, sin, w0, w1, w2, w3, w4, w5, w6, w7,
    stream_out, logits_out, small_out, send_out, keep_out, weights, sems, pgrad, whole,
):
    copies = start_weights(pos, (w0, w1, w2, w3, w4, w5, w6, w7), weights, sems)
    x, c, z, y = (pos[i] for i in range(4))
    here = 2 * x + y
    lane = iota((T, 16), 1)
    block = iota((T, T), 1) // CAP
    block_row = iota((1, T), 1) // CAP
    dispf = disp[...].astype(F32)
    g, hidden, rin = grad[...], hidden_in[...], routed[...].astype(F32)
    chances, combine = aux[:, 0:16], aux[:, 16:32]
    dots = jnp.zeros((1, T), F32)
    weight = jnp.zeros((T, T), F32)
    chance_grad = aux[:, 32:48]
    for p, r in enumerate((r0, r1, r2, r3)):
        part = r[CAP : CAP + 1, 0:T].astype(F32) + r[CAP + 1 : CAP + 2, 0:T].astype(F32)
        dots = jnp.where(block_row == p, part, dots)
        weight = jnp.where(block == p, column(combine, lane, here ^ p), weight)
    picked = dispf * dots
    for p in range(4):
        each = jnp.sum(jnp.where(block == p, picked, 0.0), axis=1, keepdims=True)
        chance_grad = chance_grad + jnp.where(lane == (here ^ p), each, 0.0)
    logit_grad = chances * (chance_grad - jnp.sum(chances * chance_grad, axis=1, keepdims=True))
    logits_out[...] = logit_grad[:, 0:NE]
    extra = aux[:, 48:64]
    mix_grad = jnp.where((lane >= 8) & (lane < 12), extra, 0.0)
    all_grad = logit_grad + mix_grad
    returned = jnp.concatenate([r[0:CAP, :] for r in (r0, r1, r2, r3)], axis=0)
    high, low = split(dispf * weight)
    smallf = small[...].astype(F32)
    routed_grad = (
        aux[:, 64:65] * g + nn(high, returned) + nn(low, returned)
        + exact(all_grad, smallf, ((1,), (0,)))
    )
    r2n = lax.rsqrt(jnp.mean(hidden * hidden, axis=1, keepdims=True) + EPSILON)
    scaled = routed_grad * smallf[15:16, :]
    hidden_grad = (
        g + r2n * scaled
        - hidden * (r2n * r2n * r2n) * jnp.mean(scaled * hidden, axis=1, keepdims=True)
    )
    attn_grad = hidden_grad.astype(BF)
    small_out[...] = exact(all_grad, rin, ((0,), (0,)))
    vector_grad = exact(jnp.where(lane >= 12, extra, 0.0), g, ((0,), (0,)))
    small_out[12:14, :] = vector_grad[12:14, :]
    small_out[15:16, :] = jnp.sum(routed_grad * hidden * r2n, axis=0, keepdims=True)
    for copy in copies:
        copy.wait()
    mixed_grad = nt(attn_grad, weights[:, 3 * D :]).astype(BF)
    whole[:, 3 * D :] = tn(mixed[...], attn_grad).astype(BF)
    first = iota((T, 128), 1) < HD
    cosine, sine = cos[...], sin[...]
    scale = 1.0 / math.sqrt(HD)
    for j in range(H // 2):
        cols = slice(j * 128, (j + 1) * 128)
        q2, k2, v2, do2 = q[:, cols], k[:, cols], v[:, cols], mixed_grad[:, cols]
        parts = []
        for hh in range(2):
            mask = first if hh == 0 else ~first
            do = jnp.where(mask, do2.astype(F32), 0.0).astype(BF)
            pb = probs[2 * j + hh]
            pf = pb.astype(F32)
            prob_grad = nt(do, v2)
            inner = jnp.sum(pf * prob_grad, axis=1, keepdims=True)
            score_grad = (pf * (prob_grad - inner)).astype(BF)
            parts.append((nn(score_grad, k2), tn(score_grad, q2), tn(pb, do2)))
        dq, dk, dv = (jnp.where(first, parts[0][n], parts[1][n]) for n in range(3))
        dq, dk = dq * scale, dk * scale
        pgrad[:, j * 128 : (j + 1) * 128] = (dq * cosine - swapped(dq) * sine).astype(BF)
        pgrad[:, D + j * 128 : D + (j + 1) * 128] = (dk * cosine - swapped(dk) * sine).astype(BF)
        pgrad[:, 2 * D + j * 128 : 2 * D + (j + 1) * 128] = dv.astype(BF)
    for n in range(9):
        cols = slice(n * 256, (n + 1) * 256)
        whole[:, cols] = tn(normed[...], pgrad[:, cols]).astype(BF)
    normed_grad = nt(pgrad[...], weights[:, : 3 * D])
    s = stream[...]
    r1n = lax.rsqrt(jnp.mean(s * s, axis=1, keepdims=True) + EPSILON)
    scaled = normed_grad * smallf[14:15, :]
    stream_out[...] = (
        hidden_grad + r1n * scaled
        - s * (r1n * r1n * r1n) * jnp.mean(scaled * s, axis=1, keepdims=True)
    )
    small_out[14:15, :] = jnp.sum(normed_grad * s * r1n, axis=0, keepdims=True)
    for p in range(4):
        at = pl.multiple_of((x ^ (p >> 1)) * WIDE, 128)
        for cr, out in enumerate((keep_out, send_out)):
            for kz in range(4):
                row = ((z ^ kz) * 2 + (y ^ (p & 1))) * ROWS + (c ^ cr) * HALF
                out[p, kz * HALF : (kz + 1) * HALF, :] = whole[
                    pl.ds(pl.multiple_of(row, 16), HALF), pl.ds(at, WIDE)
                ]


def result_body(pos, base, disp, aux, r0, r1, r2, r3, out):
    here = 2 * pos[0] + pos[3]
    lane = iota((T, 16), 1)
    block = iota((T, T), 1) // CAP
    combine = aux[:, 16:32]
    weight = jnp.zeros((T, T), F32)
    for p in range(4):
        weight = jnp.where(block == p, column(combine, lane, here ^ p), weight)
    high, low = split(disp[...].astype(F32) * weight)
    returned = jnp.concatenate([r[...] for r in (r0, r1, r2, r3)], axis=0)
    out[...] = (base[...] + nn(high, returned) + nn(low, returned)).astype(BF)


def place_body(pos, own, over, other, out):
    x, c, z, y = (pos[i] for i in range(4))
    for xr in range(2):
        for cr in range(2):
            for yr in range(2):
                for zr in range(2):
                    source = other if cr else (over if xr else own)
                    n = 2 * yr + zr + (4 * xr if cr else 0)
                    expert = 2 * (x ^ xr) + (y ^ yr)
                    quarter = 2 * ((z & 1) ^ zr) + (c ^ cr)
                    for half in range(2):
                        for o in range(2):
                            at = half * FF + quarter * QUARTER + ((y ^ yr) ^ o) * 256
                            m = 2 * half + o
                            out[expert, :, pl.ds(pl.multiple_of(at, 256), 256)] = source[
                                n, :, m * 256 : (m + 1) * 256
                            ]


def plan(mesh):
    reps, shards = mesh.shape["rep"], mesh.shape["shard"]
    spread = shards // GROUP
    assert reps == E_FFN and shards % GROUP == 0
    lows = [[hi * spread + lo for lo in range(spread)] for hi in range(GROUP)]

    def flat(rep, hi, lo):
        return rep * shards + hi * spread + lo

    def hop(value, rmask, hmask):
        pairs = [
            (flat(r, h, w), flat(r ^ rmask, h ^ hmask, w))
            for r in range(reps) for h in range(GROUP) for w in range(spread)
        ]
        return lax.ppermute(value, AXES, pairs)

    def owners(ky, up, back=False):
        pairs = []
        for r in range(reps):
            for zl in range(2):
                for y in range(2):
                    for w in range(spread):
                        source = flat(r, 2 * (2 * zl + (r & 1)) + (y ^ ky), w)
                        target = flat(r, 2 * (zl + 2 * up) + y, w)
                        pairs.append((target, source) if back else (source, target))
        return pairs

    def pick(bit, pair):
        return (jnp.where(bit == 0, pair[0], pair[1]), jnp.where(bit == 0, pair[1], pair[0]))

    XY = ((0, 0), (0, 1), (2, 0), (2, 1))
    cos_table, sin_table = tables()

    def local(
        stream, prev_logits, segments, routes, claim_order, out_cotangent,
        first_gain, attend_weight, output_weight, second_gain, router_weight,
        constant_mix, constant_vector, expert_in, expert_out,
    ):
        rep, shard = lax.axis_index("rep"), lax.axis_index("shard")
        high = shard // spread
        x, c, z, y = rep // 2, rep % 2, high // 2, high % 2
        pos = jnp.stack([x, c, z, y]).astype(I32)
        own_rows = first_gain.shape[0]

        small = jnp.concatenate(
            [router_weight, constant_mix, constant_vector, first_gain[:, None], second_gain[:, None]],
            axis=1,
        )
        small = lax.all_gather(small, "shard", axis=0, tiled=True).T

        if spread > 1:
            attend_weight, output_weight, expert_in, expert_out = (
                lax.all_gather(v, "shard", axis_index_groups=lows, axis=0, tiled=True)
                for v in (attend_weight, output_weight, expert_in, expert_out)
            )

        both = jnp.concatenate([attend_weight, output_weight], axis=1)
        mine = lax.dynamic_slice(both, (c * HALF, x * WIDE), (HALF, WIDE))
        column_part = jnp.concatenate([mine] + [hop(mine, 0, 2 * kz) for kz in (1, 2, 3)], axis=0)
        plane = [column_part] + [hop(column_part, *XY[p]) for p in (1, 2, 3)]
        pieces = []
        for p in range(4):
            pieces += [plane[p], hop(plane[p], 1, 0)]

        prev16 = jnp.concatenate([prev_logits, jnp.zeros((T, 16 - NE), F32)], axis=1)
        prev_high, prev_low = split(prev16)
        prevx = jnp.concatenate([prev_high, prev_low, jnp.zeros((T, 96), BF)], axis=1)
        *g_parts, disp = call(
            route_body,
            (shape(CAP, D + 128),) * 4 + (shape(T, T),),
            [SMEM] + [VM] * 4,
            flops=2 * T * T * 900,
            moved=2 << 20,
        )(pos, routes, claim_order, out_cotangent, prevx)

        def dispatch(parts):
            first = jnp.concatenate(
                [parts[0]] + [hop(parts[p], *XY[p]) for p in (1, 2, 3)], axis=0
            )
            second = hop(first, 0, 2)
            return first, second, hop(first, 1, 0), hop(second, 1, 0)

        g_slots = dispatch(g_parts)

        def columns(yr, zr):
            yd = y ^ yr
            quarter = 2 * ((z & 1) ^ zr) + c
            return jnp.concatenate(
                [
                    lax.dynamic_slice(
                        expert_in,
                        (0, 2 * x + yd, half * FF + quarter * QUARTER + (yd ^ o) * 256),
                        (ROWS, 1, 256),
                    )[:, 0]
                    for half in range(2) for o in range(2)
                ],
                axis=1,
            )

        across = hop(jnp.stack([columns(1, 0), columns(1, 1)]), 0, 1)
        joined = [jnp.concatenate([columns(0, zr), across[zr]], axis=0) for zr in range(2)]
        win_parts = [joined[0]] + [hop(joined[kz & 1], 0, 2 * kz) for kz in (1, 2, 3)]
        wout_parts = []
        for ky in range(2):
            rows = lax.dynamic_slice(
                expert_out, (0, 2 * x + (y ^ ky), 0), (expert_out.shape[0], 1, D)
            )[:, 0]
            for up in range(2):
                wout_parts.append(lax.ppermute(rows, AXES, owners(ky, up)))

        normed, q, k, v, probs, mixed, hidden, routed, *x_parts = call(
            attend_body,
            (shape(T, D),) * 4 + (shape(H, T, T), shape(T, D), shape(T, D, dtype=F32))
            + (shape(T, D),) + (shape(CAP, D),) * 4,
            [SMEM] + [VM] * 6 + [ANY] * 8,
            [pltpu.VMEM((D, 4 * D), BF), pltpu.SemaphoreType.DMA((32,))],
            flops=2 * T * D * 4 * D + 4 * H * T * T * 128,
            moved=10 << 20,
        )(pos, stream, small, segments, cos_table, sin_table, disp, *pieces)

        x_slots = dispatch(x_parts)

        base, aux = call(
            router_body,
            (shape(T, D, dtype=F32), shape(T, 128, dtype=F32)),
            [VM] * 6,
            flops=20 * T * D,
            moved=4 << 20,
        )(hidden, routed, small, prev16, routes, out_cotangent)

        send, keep, act, gate_up_grad, _, wout = call(
            expert_body,
            (shape(544, D), shape(544, D, dtype=F32), shape(1024, QUARTER),
             shape(1024, 2 * QUARTER), shape(D, 2 * QUARTER), shape(QUARTER, D)),
            [SMEM] + [VM] * 16,
            flops=2 * 1024 * D * 5 * QUARTER,
            moved=12 << 20,
        )(pos, *x_slots, *g_slots, *win_parts, *wout_parts)
        got = hop(send, 1, 0)
        send, keep = call(
            fold_body, (shape(272, D), shape(272, D, dtype=F32)), [VM] * 2, moved=4 << 20
        )(keep, got)
        got = hop(send, 0, 2)
        back_parts = call(spread_body, (shape(CAP + 16, D),) * 4, [VM] * 2, moved=2 << 20)(keep, got)
        back_parts = [back_parts[0]] + [hop(back_parts[p], *XY[p]) for p in (1, 2, 3)]

        out_send, out_keep = call(
            slots_out_body, (shape(512, D),) * 2, [VM] * 2, flops=2 * 1024 * QUARTER * D, moved=4 << 20
        )(act, wout)
        *win_grads, wout_grad0, wout_grad1 = call(
            weight_grad_body,
            (shape(2 * ROWS, 2 * QUARTER),) * 4 + (shape(256, D),) * 2,
            [SMEM] + [VM] * 11,
            [pltpu.VMEM((1024, 2 * QUARTER), BF), pltpu.VMEM((D, 2 * QUARTER), BF)],
            flops=2 * 1024 * D * 3 * QUARTER,
            moved=12 << 20,
        )(pos, *x_slots, *g_slots, act, gate_up_grad, small)

        stream_grad, logits_grad, small_grad, w_send, w_keep = call(
            back_body,
            (shape(T, D, dtype=F32), shape(T, NE, dtype=F32), shape(16, D, dtype=F32),
             shape(4, 4 * HALF, WIDE), shape(4, 4 * HALF, WIDE)),
            [SMEM] + [VM] * 19 + [ANY] * 8,
            [pltpu.VMEM((D, 4 * D), BF), pltpu.SemaphoreType.DMA((32,)),
             pltpu.VMEM((T, 3 * D), BF), pltpu.VMEM((D, 4 * D), BF)],
            flops=4 * T * D * 4 * D + 10 * H * T * T * 128,
            moved=24 << 20,
        )(pos, *back_parts, disp, hidden, routed, aux, out_cotangent, small, stream, normed,
          q, k, v, probs, mixed, cos_table, sin_table, *pieces)

        def add(a, b):
            return (a.astype(F32) + b.astype(F32)).astype(BF)

        out_sum = add(out_keep, hop(out_send, 1, 0))
        out_sum = add(out_sum[:256], hop(out_sum[256:], 0, 2))
        outs = [out_sum[p * CAP : (p + 1) * CAP] for p in range(4)]
        outs = [outs[0]] + [hop(outs[p], *XY[p]) for p in (1, 2, 3)]
        result = call(result_body, shape(T, D), [SMEM] + [VM] * 7, flops=4 * T * T * D, moved=3 << 20)(
            pos, base, disp, aux, *outs
        )

        arrived = [win_grads[0]] + [hop(win_grads[kz], 0, 2 * kz) for kz in (1, 2, 3)]
        sums = jnp.stack([add(arrived[0], arrived[2]), add(arrived[1], arrived[3])])
        other_y = hop(sums[:, ROWS:], 0, 1)
        own = jnp.concatenate([sums[:, :ROWS], other_y], axis=0)
        over = hop(own, 2, 0)
        other = hop(jnp.concatenate([own, over], axis=0), 1, 0)
        in_grad = call(place_body, shape(E_FFN, ROWS, 2 * FF), [SMEM] + [VM] * 3, moved=6 << 20)(
            pos, own, over, other
        )
        in_grad = in_grad.transpose(1, 0, 2).astype(F32)

        out_rows = []
        for ky, grad in enumerate((wout_grad0, wout_grad1)):
            a, b = (lax.ppermute(grad, AXES, owners(ky, up, True)) for up in range(2))
            out_rows.append(add(a, b))
        out_rows = jnp.stack(out_rows)
        out_rows = jnp.stack([out_rows, hop(out_rows, 2, 0)])
        out_rows = add(out_rows, hop(out_rows, 1, 0))
        by_x = pick(x, (out_rows[0], out_rows[1]))
        by_expert = [half for pair in by_x for half in pick(y, (pair[0], pair[1]))]
        out_grad = jnp.stack(by_expert, axis=1).astype(F32)

        total = add(w_keep, hop(w_send, 1, 0))
        parts = [total[0]] + [hop(total[p], *XY[p]) for p in (1, 2, 3)]
        total = add(add(parts[0], parts[1]), add(parts[2], parts[3]))
        parts = [total[kz * HALF : (kz + 1) * HALF] for kz in range(4)]
        parts = [parts[0]] + [hop(parts[kz], 0, 2 * kz) for kz in (1, 2, 3)]
        mine = add(add(parts[0], parts[1]), add(parts[2], parts[3]))
        wide = jnp.concatenate(pick(x, (mine, hop(mine, 2, 0))), axis=1)
        full = jnp.concatenate(pick(c, (wide, hop(wide, 1, 0))), axis=0).astype(F32)
        attend_grad, output_grad = full[:, : 3 * D], full[:, 3 * D :]

        if spread > 1:
            attend_grad, output_grad, in_grad, out_grad = (
                lax.psum_scatter(
                    v, "shard", scatter_dimension=0, axis_index_groups=lows, tiled=True
                )
                for v in (attend_grad, output_grad, in_grad, out_grad)
            )

        small_grad = lax.psum(small_grad, AXES)
        small_grad = lax.dynamic_slice(small_grad, (0, shard * own_rows), (16, own_rows))
        return (
            result,
            stream_grad,
            logits_grad,
            small_grad[14],
            attend_grad,
            output_grad,
            small_grad[15],
            small_grad[0:8].T,
            small_grad[8:12].T,
            small_grad[12:14].T,
            in_grad,
            out_grad,
        )

    return local


def solution(mesh):
    tokens = P(("rep", "shard"), None)
    weight = (P("shard"), P("shard", None), P("shard", None, None))
    return jax.shard_map(
        plan(mesh),
        mesh=mesh,
        in_specs=(tokens,) * 6
        + (weight[0], weight[1], weight[1], weight[0])
        + (weight[1],) * 3
        + (weight[2],) * 2,
        out_specs=(tokens,) * 3
        + (weight[0], weight[1], weight[1], weight[0])
        + (weight[1],) * 3
        + (weight[2],) * 2,
        check_vma=False,
    )
```

```python
import math

import jax
import jax.numpy as jnp
import numpy as np
from jax import lax
from jax.experimental import pallas as pl
from jax.experimental.pallas import tpu as pltpu
from jax.sharding import PartitionSpec as P

H = 12
HD = 64
FF = 2048
E_FFN = 4
NC = 2
NE = 8
CAP = 64
D = 768
T = 256
GROUP = 8
ROWS = D // GROUP
HALF = ROWS // 2
WIDE = 2 * D
EXTRA = 128
PACK = 576
QUARTER = FF // 4

EPSILON = 1e-06
BF = jnp.bfloat16
F32 = jnp.float32
I32 = jnp.int32
AXES = ("rep", "shard")
VMEM_LIMIT = 56 << 20


def nn(a, b):
    return lax.dot_general(a, b, (((1,), (0,)), ((), ())), preferred_element_type=F32)


def nt(a, b):
    return lax.dot_general(a, b, (((1,), (1,)), ((), ())), preferred_element_type=F32)


def tn(a, b):
    return lax.dot_general(a, b, (((0,), (0,)), ((), ())), preferred_element_type=F32)


def exact(a, b, dims):
    return lax.dot_general(
        a, b, (dims, ((), ())), precision=lax.Precision.HIGHEST, preferred_element_type=F32
    )


def iota(shape, dim):
    return lax.broadcasted_iota(I32, shape, dim)


def split(v):
    high = v.astype(BF)
    return high, (v - high.astype(F32)).astype(BF)


def tables():
    half = HD // 2
    position = np.arange(T, dtype=np.float32)
    frequency = np.exp(
        np.arange(half, dtype=np.float32) * np.float32(-2.0 * math.log(10000.0) / HD)
    ).astype(np.float32)
    angle = (position[:, None] * frequency[None, :]).astype(np.float32)
    cosine, sine = np.cos(angle), np.sin(angle)
    return (
        np.concatenate([cosine] * 4, axis=1).astype(np.float32),
        np.concatenate([-sine, sine] * 2, axis=1).astype(np.float32),
    )


def swapped(tile):
    lane = iota(tile.shape, 1) % HD
    return jnp.where(lane < HD // 2, pltpu.roll(tile, 96, 1), pltpu.roll(tile, 32, 1))


def call(body, out_shape, in_specs, scratch=(), where=pltpu.VMEM, aliases={}, ties=()):
    count = len(in_specs)

    def run(*args):
        return pl.pallas_call(
            lambda *refs: body(*refs[:count], *refs[count + len(ties) :]),
            out_shape=out_shape,
            in_specs=in_specs + [pl.BlockSpec(memory_space=pl.ANY)] * len(ties),
            out_specs=jax.tree.map(
                lambda v: pl.BlockSpec(memory_space=pltpu.SMEM if v.shape == (1,) else where),
                out_shape,
            ),
            scratch_shapes=list(scratch),
            input_output_aliases=aliases,
            compiler_params=pltpu.CompilerParams(vmem_limit_bytes=VMEM_LIMIT),
            cost_estimate=pl.CostEstimate(flops=0, bytes_accessed=0, transcendentals=0),
        )(*args, *ties)

    return run


def gate(values, others):
    count = len(values)
    return pl.pallas_call(
        lambda *refs: None,
        out_shape=[jax.ShapeDtypeStruct(v.shape, v.dtype) for v in values],
        in_specs=[pl.BlockSpec(memory_space=pl.ANY)] * (count + len(others)),
        out_specs=[pl.BlockSpec(memory_space=pl.ANY)] * count,
        input_output_aliases={n: n for n in range(count)},
    )(*values, *others)


SMEM = pl.BlockSpec(memory_space=pltpu.SMEM)
VM = pl.BlockSpec(memory_space=pltpu.VMEM)
ANY = pl.BlockSpec(memory_space=pl.ANY)


def shape(*dims, dtype=BF):
    return jax.ShapeDtypeStruct(dims, dtype)


def start_weights(pos, pieces, target, sems, extra=False):
    x, c, z, y = (pos[i] for i in range(4))
    copies = []
    for p in range(4):
        column = pl.multiple_of((x ^ (p >> 1)) * WIDE, 128)
        for cr in range(2):
            for kz in range(4):
                row = ((z ^ kz) * 2 + (y ^ (p & 1))) * ROWS + (c ^ cr) * HALF
                rows = pl.ds(pl.multiple_of(row, 16), HALF)
                piece = pieces[2 * p + cr].at[pl.ds(kz * HALF, HALF)]
                copies.append(
                    pltpu.make_async_copy(
                        piece.at[:, pl.ds(0, WIDE)],
                        target.at[rows, pl.ds(column, WIDE)],
                        sems.at[len(copies)],
                    )
                )
                if extra and p < 2:
                    copies.append(
                        pltpu.make_async_copy(
                            piece.at[:, pl.ds(WIDE, EXTRA)],
                            target.at[rows, pl.ds(2 * WIDE, EXTRA)],
                            sems.at[len(copies)],
                        )
                    )
    for copy in copies:
        copy.start()
    return copies


def group_body(pos, attend, output, router, mix, vector, gain1, gain2, out, small):
    x, c = pos[0], pos[1]
    rows = pl.ds(pl.multiple_of(c * HALF, 16), HALF)
    unit = jnp.where(iota((16, 128), 0) == iota((16, 128), 1), 1.0, 0.0).astype(BF)
    small[0:8, :], small[8:12, :], small[12:14, :] = router[...], mix[...], vector[...]
    small[14:15, :], small[15:16, :] = gain1[...], gain2[...]
    extra = tn(small[...], unit)
    out[:, WIDE:] = jnp.where(c == 0, extra[0:HALF], extra[HALF:]).astype(BF)

    @pl.when(x == 0)
    def _():
        out[:, :WIDE] = attend[rows, 0:WIDE]

    @pl.when(x == 1)
    def _():
        out[:, :D] = attend[rows, WIDE:]
        out[:, D:WIDE] = output[rows, :]


def expert_at_body(pos, out):
    out[0] = 2 * pos[0] + pos[3]


def cut_body(pos, ein, eout, near, far):
    c, z = pos[1], pos[2]
    lane = iota((ROWS, 128), 1)
    for zr in range(2):
        low, target, base = (z & 1) ^ zr, (near, far)[zr], 0
        for half in range(2):
            for t in range(4):
                a, b = (
                    ein[:, pl.ds(pl.multiple_of((half * 16 + 4 * t + 2 * o + low) * 128, 128), 128)]
                    .astype(F32) for o in range(2)
                )
                first = jnp.where(c == 0, a, pltpu.roll(a, 64, 1))
                second = jnp.where(c == 0, pltpu.roll(b, 64, 1), b)
                m, cols = 2 * half + t // 2, slice((t % 2) * 128, (t % 2 + 1) * 128)
                target[base + m * ROWS : base + (m + 1) * ROWS, cols] = jnp.where(
                    lane < 64, first, second
                ).astype(BF)
        row = pl.multiple_of((2 * low + c) * 64, 64)
        for n in range(3):
            at = base + 4 * ROWS + n * 64
            target[at : at + 64, :] = eout[pl.ds(row, 64), n * 256 : (n + 1) * 256]

def attend_body(
    pos, stream, seg, cos, sin, disp, w0, w1, w2, w3, w4, w5, w6, w7,
    normed_out, q_out, k_out, v_out, probs_out, mixed_out, hidden_out, routed_out, small_out,
    x0, x1, x2, x3, weights, sems,
):
    copies = start_weights(pos, (w0, w1, w2, w3, w4, w5, w6, w7), weights, sems, extra=True)
    s = stream[...]
    r1 = lax.rsqrt(jnp.mean(s * s, axis=1, keepdims=True) + EPSILON)
    row, col = iota((T, T), 0), iota((T, T), 1)
    segf = seg[...].astype(F32)
    segcol = jnp.sum(jnp.where(row == col, segf, 0.0), axis=1, keepdims=True)
    allowed = (segcol == segf) & (col <= row)
    cosine, sine = cos[...], sin[...]
    for copy in copies:
        copy.wait()
    small = jnp.transpose(weights[:, 2 * WIDE :].astype(F32))[0:16]
    small_out[...] = small.astype(BF)
    normed = (s * r1 * small[14:15, :]).astype(BF)
    normed_out[...] = normed
    for n in range(9):
        part = nn(normed, weights[:, n * 256 : (n + 1) * 256])
        out, base = (q_out, k_out, v_out)[n // 3], (n % 3) * 256
        for t in range(2):
            tile = part[:, t * 128 : (t + 1) * 128]
            if n < 6:
                tile = tile * cosine + swapped(tile) * sine
            out[:, base + t * 128 : base + (t + 1) * 128] = tile.astype(BF)
    first = iota((T, 128), 1) < HD
    for j in range(H // 2):
        cols = slice(j * 128, (j + 1) * 128)
        q2, k2, v2 = q_out[:, cols], k_out[:, cols], v_out[:, cols]
        halves = []
        for hh in range(2):
            mask = first if hh == 0 else ~first
            qm = jnp.where(mask, q2.astype(F32), 0.0).astype(BF)
            scores = jnp.where(allowed, nt(qm, k2) * (1.0 / math.sqrt(HD)), -1e30)
            raised = jnp.exp(scores - jnp.max(scores, axis=1, keepdims=True))
            probs = (raised / jnp.sum(raised, axis=1, keepdims=True)).astype(BF)
            probs_out[2 * j + hh] = probs
            halves.append(nn(probs, v2))
        mixed_out[:, cols] = jnp.where(first, halves[0], halves[1]).astype(BF)
    hidden = s + nn(mixed_out[...], weights[:, 3 * D : 4 * D])
    hidden_out[...] = hidden
    r2 = lax.rsqrt(jnp.mean(hidden * hidden, axis=1, keepdims=True) + EPSILON)
    routed = (hidden * r2 * small[15:16, :]).astype(BF)
    routed_out[...] = routed
    slots = tn(disp[...], routed).astype(BF)
    for p, out in enumerate((x0, x1, x2, x3)):
        out[...] = slots[p * CAP : (p + 1) * CAP]


def route_body(pos, routes, order, grad, prev, g0, g1, g2, g3, disp_out, meta_out, flipped):
    here = 2 * pos[0] + pos[3]
    row, col = iota((T, T), 0), iota((T, T), 1)
    lane = iota((T, 128), 1)
    flipped[...] = jnp.zeros((128, T), F32)
    flipped[0:NE, :] = prev[...]
    flipped[NE : NE + 2, :] = routes[...].astype(F32)
    meta = jnp.transpose(flipped[...])
    meta_out[...] = meta
    lanef = lane.astype(F32)
    first, second = meta[:, NE : NE + 1], meta[:, NE + 1 : NE + 2]
    chosen = ((first == lanef) | (second == lanef)) & (lane < E_FFN)
    claims = jnp.where(order[...] == row, 1.0, 0.0).astype(BF)
    ranked = tn(claims, jnp.where(chosen, 1.0, 0.0).astype(BF))
    before = nn(jnp.where(col < row, 1.0, 0.0).astype(BF), ranked.astype(BF))
    place = nn(claims, before.astype(BF))
    kept = chosen & (place < CAP)
    dispatch = jnp.zeros((T, T), F32)
    colf = col.astype(F32)
    for p in range(4):
        mine = kept & (lane == (here ^ p))
        target = jnp.sum(jnp.where(mine, place + (p * CAP + 1.0), 0.0), axis=1, keepdims=True)
        dispatch = dispatch + jnp.where(colf == target - 1.0, 1.0, 0.0)
    dispatch = dispatch.astype(BF)
    disp_out[...] = dispatch
    slots = tn(dispatch, grad[...].astype(BF)).astype(BF)
    high, low = split(jnp.where(lane < NE, meta, 0.0))
    extra = tn(dispatch, high), pltpu.roll(tn(dispatch, low), 16, 1)
    extra = (extra[0] + extra[1]).astype(BF)
    for p, out in enumerate((g0, g1, g2, g3)):
        out[:, :D] = slots[p * CAP : (p + 1) * CAP]
        out[:, D:] = extra[p * CAP : (p + 1) * CAP]


def column(v, lane, index):
    return jnp.sum(jnp.where(lane == index, v, 0.0), axis=1, keepdims=True)


def chance(logits, lane):
    masked = jnp.where(lane < NE, logits, -1e30)
    raised = jnp.where(lane < NE, jnp.exp(masked - jnp.max(masked, axis=1, keepdims=True)), 0.0)
    return raised / jnp.sum(raised, axis=1, keepdims=True)


def router_body(hidden, routed, small, meta, grad, base_out, aux_out):
    lane = iota((T, 16), 1)
    rin = routed[...].astype(F32)
    g = grad[...]
    logits = nt(routed[...], small[...])
    chances = chance(logits + jnp.where(lane < NE, meta[:, 0:16], 0.0), lane)
    lanef = lane.astype(F32)
    chosen = (meta[:, NE : NE + 1] == lanef) | (meta[:, NE + 1 : NE + 2] == lanef)
    combine = jnp.where(chosen, chances, 0.0)
    copy_weight = column(combine, lane, E_FFN + 1)
    copy_grad = jnp.sum(g * rin, axis=1, keepdims=True)
    base = hidden[...] + copy_weight * rin
    others = jnp.where(lane == E_FFN + 1, copy_grad, 0.0)
    mixing_grad = jnp.zeros((T, 16), F32)
    factor = copy_weight
    for n in range(NC):
        l0, l1 = column(logits, lane, 8 + 2 * n), column(logits, lane, 9 + 2 * n)
        a0, a1 = 1.0 / (1.0 + jnp.exp(l1 - l0)), 1.0 / (1.0 + jnp.exp(l0 - l1))
        vector = small[12 + n : 13 + n, :].astype(F32)
        weight = column(combine, lane, E_FFN + 2 + n)
        base = base + weight * (a0 * rin + a1 * vector)
        vector_dot = jnp.sum(g * vector, axis=1, keepdims=True)
        others = others + jnp.where(
            lane == E_FFN + 2 + n, a0 * copy_grad + a1 * vector_dot, 0.0
        )
        d0, d1 = weight * copy_grad, weight * vector_dot
        total = a0 * d0 + a1 * d1
        mixing_grad = mixing_grad + jnp.where(lane == 8 + 2 * n, a0 * (d0 - total), 0.0)
        mixing_grad = mixing_grad + jnp.where(lane == 9 + 2 * n, a1 * (d1 - total), 0.0)
        mixing_grad = mixing_grad + jnp.where(lane == 12 + n, a1 * weight, 0.0)
        factor = factor + a0 * weight
    base_out[...] = base
    aux_out[:, 0:16] = chances
    aux_out[:, 16:32] = combine
    aux_out[:, 32:48] = jnp.where(chosen, others, 0.0)
    aux_out[:, 48:64] = mixing_grad
    aux_out[:, 64:128] = jnp.broadcast_to(factor, (T, 64))


def expert_body(
    pos, x0, x1, x2, x3, g0, g1, g2, v0, v1, v2, v3, v4, v5,
    send_out, keep_out, act_out, grad_out, win_out, wout_out,
):
    z, y = pos[2], pos[3]
    near, far = pl.ds(0, PACK), pl.ds(PACK, PACK)
    pieces = (v0, v1, v2.at[near], v2.at[far], v3.at[near], v3.at[far], v4, v5)
    for n, piece in enumerate(pieces):
        shard = (z ^ (n // 2)) * 2 + (y ^ (n % 2))
        row = pl.multiple_of(shard * ROWS, 16)
        for m in range(4):
            win_out[pl.ds(row, ROWS), m * 256 : (m + 1) * 256] = piece[m * ROWS : (m + 1) * ROWS, :]
        row = pl.multiple_of(shard * 64, 64)
        for m in range(3):
            wout_out[pl.ds(row, 64), m * 256 : (m + 1) * 256] = piece[
                4 * ROWS + m * 64 : 4 * ROWS + (m + 1) * 64, :
            ]
    win, wout = win_out[...], wout_out[...]
    ones = jnp.ones((16, QUARTER), F32)
    grads = (g0[:, :D], g1[:, :D], g2[0:256, :D], g2[256:512, :D])
    for b, (xs, gs) in enumerate(zip((x0, x1, x2, x3), grads)):
        rows = slice(b * 256, (b + 1) * 256)
        gate_up = nn(xs[...], win)
        a, u = gate_up[:, :QUARTER], gate_up[:, QUARTER:]
        sigma = 1.0 / (1.0 + jnp.exp(-a))
        swish = a * sigma
        activated = (swish * u).astype(BF)
        act_out[rows, :] = activated
        back = nt(gs, wout)
        dots = exact(ones, activated.astype(F32) * back, ((1,), (1,)))[0:1]
        gate_grad = back * u * sigma * (1.0 + a * (1.0 - sigma))
        both = jnp.concatenate([gate_grad.astype(BF), (back * swish).astype(BF)], axis=1)
        grad_out[rows, :] = both
        slot_grad = nt(both, win)
        at = (b % 2) * 272
        if b < 2:
            keep_out[at : at + 256, :] = slot_grad
            keep_out[at + 256 : at + 272, :] = jnp.zeros((16, D), F32)
            keep_out[at + 256 : at + 257, 0:256] = dots
        else:
            high, low = split(dots)
            send_out[at : at + 256, :] = slot_grad.astype(BF)
            send_out[at + 256 : at + 272, :] = jnp.zeros((16, D), BF)
            send_out[at + 256 : at + 258, 0:256] = jnp.concatenate([high, low], axis=0)


def fold_body(keep, got, send_out, keep_out):
    total = keep[...] + got[...].astype(F32)
    dots = [keep[n * 272 + 256 : n * 272 + 257, 0:256]
            + got[n * 272 + 256 : n * 272 + 257, 0:256].astype(F32)
            + got[n * 272 + 257 : n * 272 + 258, 0:256].astype(F32) for n in range(2)]
    keep_out[0:256, :] = total[0:256]
    keep_out[256:272, :] = jnp.zeros((16, D), F32)
    keep_out[256:257, 0:256] = dots[0]
    high, low = split(dots[1])
    send_out[0:256, :] = total[272:528].astype(BF)
    send_out[256:272, :] = jnp.zeros((16, D), BF)
    send_out[256:258, 0:256] = jnp.concatenate([high, low], axis=0)


def spread_body(keep, got, r0, r1, r2, r3):
    total = (keep[0:256, :] + got[0:256, :].astype(F32)).astype(BF)
    dots = (
        keep[256:257, 0:256] + got[256:257, 0:256].astype(F32) + got[257:258, 0:256].astype(F32)
    )
    high, low = split(dots)
    for p, out in enumerate((r0, r1, r2, r3)):
        out[0:CAP, :] = total[p * CAP : (p + 1) * CAP]
        out[CAP : CAP + 16, :] = jnp.zeros((16, D), BF)
        out[CAP : CAP + 2, 0:256] = jnp.concatenate([high, low], axis=0)


def slots_out_body(act, wout, send_out, keep_out):
    for b in range(4):
        part = nn(act[b * 256 : (b + 1) * 256, :], wout[...]).astype(BF)
        out = (keep_out, send_out)[b // 2]
        out[(b % 2) * 256 : (b % 2 + 1) * 256, :] = part


def weight_grad_body(
    pos, x0, x1, x2, x3, g0, g1, g2, act, grad, small,
    d0, d1, d2, d3, scaled, whole, rows_out,
):
    x, z, y = pos[0], pos[2], pos[3]
    lane = iota((256, 16), 1)
    expert = 2 * x + y
    total = jnp.zeros((QUARTER, D), F32)
    xs = jnp.concatenate([v[...] for v in (x0, x1, x2, x3)], axis=0)
    grads = (g0[...], g1[...], g2[0:256, :], g2[256:512, :])
    for b, (xv, gs) in enumerate(zip((x0, x1, x2, x3), grads)):
        rows = slice(b * 256, (b + 1) * 256)
        prev = gs[:, D : D + 16].astype(F32) + gs[:, D + 16 : D + 32].astype(F32)
        chances = chance(nt(xv[...], small[...]) + jnp.where(lane < NE, prev, 0.0), lane)
        weight = column(chances, lane, expert)
        scaled[rows, :] = (grad[rows, :].astype(F32) * weight).astype(BF)
        total = total + tn(act[rows, :], (gs[:, :D].astype(F32) * weight).astype(BF))
    rows_out[...] = total.astype(BF)
    for n in range(4):
        cols = slice(n * 256, (n + 1) * 256)
        whole[:, cols] = tn(xs, scaled[:, cols]).astype(BF)
    for n in range(8):
        out, base = (d0, d1, d2, d3)[n // 2], (n % 2) * PACK
        shard = (z ^ (n // 2)) * 2 + (y ^ (n % 2))
        row = pl.multiple_of(shard * ROWS, 16)
        for m in range(4):
            out[base + m * ROWS : base + (m + 1) * ROWS, :] = whole[
                pl.ds(row, ROWS), m * 256 : (m + 1) * 256
            ]
        row, base = pl.multiple_of(shard * 64, 64), base + 4 * ROWS
        for m in range(3):
            out[base + m * 64 : base + (m + 1) * 64, :] = rows_out[
                pl.ds(row, 64), m * 256 : (m + 1) * 256
            ]


def back_body(
    pos, r0, r1, r2, r3, disp, hidden_in, routed, aux, grad, small, stream, normed, q, k, v,
    probs, mixed, cos, sin, w0, w1, w2, w3, w4, w5, w6, w7,
    stream_out, logits_out, ka, kb, kc, kd, sa, sb, sc, sd, weights, sems, pgrad, whole, small_out,
):
    copies = start_weights(pos, (w0, w1, w2, w3, w4, w5, w6, w7), weights, sems)
    x, c, z, y = (pos[i] for i in range(4))
    here = 2 * x + y
    lane = iota((T, 16), 1)
    block = iota((T, T), 1) // CAP
    block_row = iota((1, T), 1) // CAP
    dispf = disp[...].astype(F32)
    g, hidden, rin = grad[...], hidden_in[...], routed[...].astype(F32)
    chances, combine = aux[:, 0:16], aux[:, 16:32]
    dots = jnp.zeros((1, T), F32)
    weight = jnp.zeros((T, T), F32)
    chance_grad = aux[:, 32:48]
    for p, r in enumerate((r0, r1, r2, r3)):
        part = r[CAP : CAP + 1, 0:T].astype(F32) + r[CAP + 1 : CAP + 2, 0:T].astype(F32)
        dots = jnp.where(block_row == p, part, dots)
        weight = jnp.where(block == p, column(combine, lane, here ^ p), weight)
    picked = dispf * dots
    for p in range(4):
        each = jnp.sum(jnp.where(block == p, picked, 0.0), axis=1, keepdims=True)
        chance_grad = chance_grad + jnp.where(lane == (here ^ p), each, 0.0)
    logit_grad = chances * (chance_grad - jnp.sum(chances * chance_grad, axis=1, keepdims=True))
    logits_out[...] = jnp.transpose(logit_grad)[0:NE]
    extra = aux[:, 48:64]
    mix_grad = jnp.where((lane >= 8) & (lane < 12), extra, 0.0)
    all_grad = logit_grad + mix_grad
    returned = jnp.concatenate([r[0:CAP, :] for r in (r0, r1, r2, r3)], axis=0)
    high, low = split(dispf * weight)
    smallf = small[...].astype(F32)
    routed_grad = (
        aux[:, 64:65] * g + nn(high, returned) + nn(low, returned)
        + exact(all_grad, smallf, ((1,), (0,)))
    )
    r2n = lax.rsqrt(jnp.mean(hidden * hidden, axis=1, keepdims=True) + EPSILON)
    scaled = routed_grad * smallf[15:16, :]
    hidden_grad = (
        g + r2n * scaled
        - hidden * (r2n * r2n * r2n) * jnp.mean(scaled * hidden, axis=1, keepdims=True)
    )
    attn_grad = hidden_grad.astype(BF)
    small_out[...] = jnp.zeros((EXTRA, D), F32)
    small_out[0:16, :] = exact(all_grad, rin, ((0,), (0,)))
    vector_grad = exact(jnp.where(lane >= 12, extra, 0.0), g, ((0,), (0,)))
    small_out[12:14, :] = vector_grad[12:14, :]
    small_out[15:16, :] = jnp.sum(routed_grad * hidden * r2n, axis=0, keepdims=True)
    for copy in copies:
        copy.wait()
    mixed_grad = nt(attn_grad, weights[:, 3 * D :]).astype(BF)
    whole[:, 3 * D : 4 * D] = tn(mixed[...], attn_grad).astype(BF)
    first = iota((T, 128), 1) < HD
    cosine, sine = cos[...], sin[...]
    scale = 1.0 / math.sqrt(HD)
    for j in range(H // 2):
        cols = slice(j * 128, (j + 1) * 128)
        q2, k2, v2, do2 = q[:, cols], k[:, cols], v[:, cols], mixed_grad[:, cols]
        parts = []
        for hh in range(2):
            mask = first if hh == 0 else ~first
            do = jnp.where(mask, do2.astype(F32), 0.0).astype(BF)
            pb = probs[2 * j + hh]
            pf = pb.astype(F32)
            prob_grad = nt(do, v2)
            inner = jnp.sum(pf * prob_grad, axis=1, keepdims=True)
            score_grad = (pf * (prob_grad - inner)).astype(BF)
            parts.append((nn(score_grad, k2), tn(score_grad, q2), tn(pb, do2)))
        dq, dk, dv = (jnp.where(first, parts[0][n], parts[1][n]) for n in range(3))
        dq, dk = dq * scale, dk * scale
        pgrad[:, j * 128 : (j + 1) * 128] = (dq * cosine - swapped(dq) * sine).astype(BF)
        pgrad[:, D + j * 128 : D + (j + 1) * 128] = (dk * cosine - swapped(dk) * sine).astype(BF)
        pgrad[:, 2 * D + j * 128 : 2 * D + (j + 1) * 128] = dv.astype(BF)
    for n in range(9):
        cols = slice(n * 256, (n + 1) * 256)
        whole[:, cols] = tn(normed[...], pgrad[:, cols]).astype(BF)
    normed_grad = nt(pgrad[...], weights[:, : 3 * D])
    s = stream[...]
    r1n = lax.rsqrt(jnp.mean(s * s, axis=1, keepdims=True) + EPSILON)
    scaled = normed_grad * smallf[14:15, :]
    stream_out[...] = (
        hidden_grad + r1n * scaled
        - s * (r1n * r1n * r1n) * jnp.mean(scaled * s, axis=1, keepdims=True)
    )
    small_out[14:15, :] = jnp.sum(normed_grad * s * r1n, axis=0, keepdims=True)
    whole[:, 2 * WIDE :] = jnp.transpose(small_out[...]).astype(BF)
    for p in range(4):
        at = pl.multiple_of((x ^ (p >> 1)) * WIDE, 128)
        for cr, out in enumerate(((ka, kb, kc, kd)[p], (sa, sb, sc, sd)[p])):
            for kz in range(4):
                row = ((z ^ kz) * 2 + (y ^ (p & 1))) * ROWS + (c ^ cr) * HALF
                rows, to = pl.ds(pl.multiple_of(row, 16), HALF), slice(kz * HALF, (kz + 1) * HALF)
                out[to, 0:WIDE] = whole[rows, pl.ds(at, WIDE)]
                extra = whole[rows, 2 * WIDE :]
                out[to, WIDE:] = jnp.where((x ^ (p >> 1)) == 0, extra, jnp.zeros_like(extra))


def add_body(k0, k1, k2, k3, g0, g1, g2, g3, o0, o1, o2, o3):
    for keep, got, out in ((k0, g0, o0), (k1, g1, o1), (k2, g2, o2), (k3, g3, o3)):
        out[...] = (keep[...].astype(F32) + got[...].astype(F32)).astype(BF)


def result_body(pos, base, disp, aux, r0, r1, r2, r3, out):
    here = 2 * pos[0] + pos[3]
    lane = iota((T, 16), 1)
    block = iota((T, T), 1) // CAP
    combine = aux[:, 16:32]
    weight = jnp.zeros((T, T), F32)
    for p in range(4):
        weight = jnp.where(block == p, column(combine, lane, here ^ p), weight)
    high, low = split(disp[...].astype(F32) * weight)
    returned = jnp.concatenate([r[...] for r in (r0, r1, r2, r3)], axis=0)
    out[...] = (base[...] + nn(high, returned) + nn(low, returned)).astype(BF)


def finish_body(
    pos, own, over, got, got_over,
    attend_out, output_out, router_out, mix_out, vector_out, gain1_out, gain2_out, extra,
):
    x, c = pos[0], pos[1]
    for cr, (near, far) in enumerate(((own, over), (got, got_over))):
        rows = pl.ds(pl.multiple_of((c ^ cr) * HALF, 16), HALF)
        a, b = near[...].astype(F32), far[...].astype(F32)
        first, second = jnp.where(x == 0, a, b), jnp.where(x == 0, b, a)
        attend_out[rows, 0:WIDE] = first[:, :WIDE]
        attend_out[rows, WIDE:] = second[:, :D]
        output_out[rows, :] = second[:, D:WIDE]
        extra[rows, :] = first[:, WIDE:]
    extra[ROWS:, :] = jnp.zeros((128 - ROWS, 128), F32)
    small = jnp.transpose(extra[...])[0:16, 0:ROWS]
    router_out[...], mix_out[...], vector_out[...] = small[0:8], small[8:12], small[12:14]
    gain1_out[...], gain2_out[...] = small[14:15], small[15:16]


def place_copies(pos, zr, blocks, in_out, out_out, ins, outs, sems, mine, theirs):
    x, c, z, y = (pos[i] for i in range(4))
    here = 2 * x + y
    lane = iota((ROWS, 128), 1)
    low = (z & 1) ^ zr
    for target, parts in ((mine, blocks[:2]), (theirs, blocks[2:])):
        target[: 2 * PACK, :], target[2 * PACK :, :] = parts[0][...], parts[1][...]
    copies = []
    for half in range(2):
        for s in range(8):
            m, cols = 2 * half + s // 4, slice((s % 4) // 2 * 128, ((s % 4) // 2 + 1) * 128)
            n = 8 * half + s
            for expert in range(E_FFN):
                rows = pl.ds(pl.multiple_of((expert ^ here) * PACK + m * ROWS, 16), ROWS)
                a, b = mine[rows, cols].astype(F32), theirs[rows, cols].astype(F32)
                first, second = jnp.where(c == 0, a, b), jnp.where(c == 0, b, a)
                if s % 2:
                    first = pltpu.roll(first, HD, 1)
                else:
                    second = pltpu.roll(second, HD, 1)
                ins[n, :, expert, :] = jnp.where(lane < HD, first, second)
            tile = pl.multiple_of((half * 16 + 2 * s + low) * 128, 128)
            copies.append(
                pltpu.make_async_copy(ins.at[n], in_out.at[:, :, pl.ds(tile, 128)], sems.at[n])
            )
            copies[-1].start()
    for cr, source in enumerate((mine, theirs)):
        for expert in range(E_FFN):
            for n in range(3):
                rows = pl.ds(
                    pl.multiple_of((expert ^ here) * PACK + 4 * ROWS + n * 64, 16), 64
                )
                outs[cr, :, expert, n * 256 : (n + 1) * 256] = source[rows, :].astype(F32)
        row = (2 * low + (c ^ cr)) * 64
        copies.append(
            pltpu.make_async_copy(outs.at[cr], out_out.at[pl.ds(row, 64)], sems.at[16 + cr])
        )
        copies[-1].start()
    for copy in copies:
        copy.wait()


def place_first_body(pos, b0, b1, b2, b3, *rest):
    place_copies(pos, 0, (b0, b1, b2, b3), *rest)


def place_second_body(pos, b0, b1, b2, b3, in_old, out_old, *rest):
    place_copies(pos, 1, (b0, b1, b2, b3), *rest)


def plan(mesh):
    reps, shards = mesh.shape["rep"], mesh.shape["shard"]
    spread = shards // GROUP
    assert reps == E_FFN and shards % GROUP == 0
    lows = [[hi * spread + lo for lo in range(spread)] for hi in range(GROUP)]

    def flat(rep, hi, lo):
        return rep * shards + hi * spread + lo

    def hop(value, rmask, hmask):
        pairs = [
            (flat(r, h, w), flat(r ^ rmask, h ^ hmask, w))
            for r in range(reps) for h in range(GROUP) for w in range(spread)
        ]
        return lax.ppermute(value, AXES, pairs)

    XY = ((0, 0), (0, 1), (2, 0), (2, 1))

    def exchange(parts):
        return [parts[0]] + [hop(parts[p], *XY[p]) for p in (1, 2, 3)]

    def relay(parts):
        n = parts[0].shape[0]
        by_y = hop(jnp.concatenate([parts[1], parts[3]], axis=0), 0, 1)
        by_x = hop(jnp.concatenate([parts[2], by_y[n:]], axis=0), 2, 0)
        return [parts[0], by_y[:n], by_x[:n], by_x[n:]]

    def line(parts):
        return [parts[0]] + [hop(parts[kz], 0, 2 * kz) for kz in (1, 2, 3)]

    def after(value, *others):
        return gate([value], others)[0]

    def add(a, b):
        return (a.astype(F32) + b.astype(F32)).astype(BF)

    cos_table, sin_table = tables()
    place_scratch = [
        pltpu.VMEM((16, ROWS, E_FFN, 128), F32),
        pltpu.VMEM((2, 64, E_FFN, D), F32),
        pltpu.SemaphoreType.DMA((18,)),
        pltpu.VMEM((4 * PACK, 256), BF),
        pltpu.VMEM((4 * PACK, 256), BF),
    ]

    def local(
        stream, prev_logits, segments, routes, claim_order, out_cotangent,
        first_gain, attend_weight, output_weight, second_gain, router_weight,
        constant_mix, constant_vector, expert_in, expert_out,
    ):
        rep, shard = lax.axis_index("rep"), lax.axis_index("shard")
        high = shard // spread
        x, c, z, y = rep // 2, rep % 2, high // 2, high % 2
        pos = jnp.stack([x, c, z, y]).astype(I32)

        smalls = [router_weight.T, constant_mix.T, constant_vector.T, first_gain[None], second_gain[None]]
        if spread > 1:
            smalls = [
                lax.all_gather(v, "shard", axis_index_groups=lows, axis=1, tiled=True) for v in smalls
            ]
            attend_weight, output_weight, expert_in, expert_out = (
                lax.all_gather(v, "shard", axis_index_groups=lows, axis=0, tiled=True)
                for v in (attend_weight, output_weight, expert_in, expert_out)
            )

        def cut(at):
            ein = lax.dynamic_slice(expert_in, (0, at[0], 0), (ROWS, 1, 2 * FF))[:, 0]
            eout = lax.dynamic_slice(expert_out, (0, at[0], 0), (FF // GROUP, 1, D))[:, 0]
            return call(cut_body, (shape(PACK, 256),) * 2, [SMEM] + [VM] * 2)(pos, ein, eout)

        *g_parts, disp, meta = call(
            route_body,
            (shape(CAP, D + 128),) * 4 + (shape(T, T), shape(T, 128, dtype=F32)),
            [SMEM] + [VM] * 4,
            [pltpu.VMEM((128, T), F32)],
        )(pos, routes.T, claim_order, out_cotangent, prev_logits.T)
        g_first = jnp.concatenate(relay(g_parts), axis=0)

        mine = call(
            group_body,
            shape(HALF, WIDE + EXTRA),
            [SMEM] + [VM] * 7,
            [pltpu.VMEM((16, ROWS), BF)],
            ties=(disp,),
        )(pos, attend_weight, output_weight, *smalls)
        w_lines = line([mine] * 4)
        w_column = jnp.concatenate(w_lines, axis=0)

        cut_across = cut([2 * x + (y ^ 1)])
        came = hop(jnp.concatenate(cut_across, axis=0), 0, 1)
        came = came[:PACK], came[PACK:]
        w_column, = gate([w_column], [g_first])
        cut_own = cut(
            call(expert_at_body, shape(1, dtype=I32), [SMEM], ties=(w_column, cut_across[0]))(pos)
        )
        plane = [w_column] + [hop(w_column, *XY[p]) for p in (1, 2, 3)]
        pieces = [v for p in range(4) for v in (plane[p], hop(plane[p], 1, 0))]
        part_2 = hop(jnp.concatenate([cut_own[0], came[0]], axis=0), 0, 4)
        g_second = hop(g_first, 0, 2)

        normed, q, k, v, probs, mixed, hidden, routed, small, *x_parts = call(
            attend_body,
            (shape(T, D),) * 4 + (shape(H, T, T), shape(T, D), shape(T, D, dtype=F32))
            + (shape(T, D), shape(16, D)) + (shape(CAP, D),) * 4,
            [SMEM] + [VM] * 5 + [ANY] * 8,
            [pltpu.VMEM((D, 4 * D + EXTRA), BF), pltpu.SemaphoreType.DMA((48,))],
            ties=(part_2, g_second),
        )(pos, stream, segments, cos_table, sin_table, disp, *pieces)
        part_30 = hop(after(cut_own[1], part_2), 0, 6)
        part_1 = hop(gate([jnp.concatenate([cut_own[1], came[1]], axis=0)], [part_2])[0], 0, 2)
        x_first = jnp.concatenate(exchange(x_parts), axis=0)
        x_first, = gate([x_first], [part_30, part_1])
        part_31 = hop(after(came[1], part_30), 0, 6)
        x_second, x_third = hop(x_first, 0, 2), hop(x_first, 1, 0)
        g_other = hop(jnp.concatenate([g_first, g_second], axis=0), 1, 0)
        base, aux = call(
            router_body, (shape(T, D, dtype=F32), shape(T, 128, dtype=F32)), [VM] * 5
        )(hidden, routed, small, meta, out_cotangent)
        x_second, = gate([x_second], [aux, part_31])
        x_slots = (x_first, x_second, x_third, hop(x_second, 1, 0))
        g_slots = (g_first, g_second, g_other)
        expert_parts = (cut_own[0], came[0], part_1, part_2, part_30, part_31)

        send, keep, act, gate_up_grad, _, wout = call(
            expert_body,
            (shape(544, D), shape(544, D, dtype=F32), shape(1024, QUARTER),
             shape(1024, 2 * QUARTER), shape(D, 2 * QUARTER), shape(QUARTER, D)),
            [SMEM] + [VM] * 13,
        )(pos, *x_slots, *g_slots, *expert_parts)
        got = hop(send, 1, 0)
        out_send, out_keep = call(slots_out_body, (shape(512, D),) * 2, [VM] * 2)(act, wout)
        send, keep = call(
            fold_body, (shape(272, D), shape(272, D, dtype=F32)), [VM] * 2, ties=(out_keep,)
        )(keep, got)
        got, out_got = hop(send, 0, 2), hop(out_send, 1, 0)
        grad_parts = call(
            weight_grad_body,
            (shape(2 * PACK, 256),) * 4,
            [SMEM] + [VM] * 10,
            [pltpu.VMEM((1024, 2 * QUARTER), BF), pltpu.VMEM((D, 2 * QUARTER), BF),
             pltpu.VMEM((QUARTER, D), BF)],
            ties=(keep,),
        )(pos, *x_slots, *g_slots, act, gate_up_grad, small)
        back_parts = call(
            spread_body, (shape(CAP + 16, D),) * 4, [VM] * 2, ties=(grad_parts[0], out_got)
        )(keep, got)
        out_sum = add(out_keep, out_got)
        part_1, part_2 = gate([grad_parts[1], grad_parts[2]], [got])
        out_half, = gate([out_sum[256:]], [back_parts[0]])
        grad_1, grad_2, out_half = hop(part_1, 0, 2), hop(part_2, 0, 4), hop(out_half, 0, 2)
        back_parts = exchange(back_parts)

        stream_grad, logits_grad, *w_parts = call(
            back_body,
            (shape(T, D, dtype=F32), shape(NE, T, dtype=F32))
            + (shape(4 * HALF, WIDE + EXTRA),) * 8,
            [SMEM] + [VM] * 19 + [ANY] * 8,
            [pltpu.VMEM((D, 4 * D), BF), pltpu.SemaphoreType.DMA((32,)),
             pltpu.VMEM((T, 3 * D), BF), pltpu.VMEM((D, 4 * D + EXTRA), BF),
             pltpu.VMEM((EXTRA, D), F32)],
        )(pos, *back_parts, disp, hidden, routed, aux, out_cotangent, small, stream, normed,
          q, k, v, probs, mixed, cos_table, sin_table, *pieces)

        w_sums = call(
            add_body, (shape(4 * HALF, WIDE + EXTRA),) * 4, [VM] * 8
        )(*w_parts[:4], *(hop(v, 1, 0) for v in w_parts[4:]))
        w_sums_near = w_sums[0]
        w_sums = exchange(w_sums)
        grad_3 = hop(gate([grad_parts[3]], [w_sums_near])[0], 0, 6)
        out_sum = add(out_sum[:256], out_half)
        w_total = add(add(w_sums[0], w_sums[1]), add(w_sums[2], w_sums[3]))

        def swap(near, across):
            both = jnp.concatenate([near, hop(across, 0, 1)], axis=0)
            far = hop(both, 2, 0)
            return both, far, hop(both, 1, 0), hop(far, 1, 0)

        sum_0 = add(grad_parts[0], grad_2)
        blocks_0 = swap(sum_0[:PACK], sum_0[PACK:])

        w_total, = gate([w_total], [grad_3, *blocks_0])
        out_sum, = gate([out_sum], [w_total])
        outs = relay([out_sum[p * CAP : (p + 1) * CAP] for p in range(4)])
        result = call(result_body, shape(T, D), [SMEM] + [VM] * 7)(pos, base, disp, aux, *outs)
        w_lines = line([w_total[kz * HALF : (kz + 1) * HALF] for kz in range(4)])
        own = add(add(w_lines[0], w_lines[1]), add(w_lines[2], w_lines[3]))
        sum_1 = add(grad_1, grad_3)
        blocks_1 = swap(sum_1[:PACK], sum_1[PACK:])
        placed = call(
            place_first_body,
            (shape(ROWS, E_FFN, 2 * FF, dtype=F32), shape(FF // GROUP, E_FFN, D, dtype=F32)),
            [SMEM] + [VM] * 4,
            place_scratch,
            where=pl.ANY,
        )(pos, *blocks_0)
        own, = gate([own], [placed[0]])
        over, got = hop(own, 2, 0), hop(own, 1, 0)
        got_over = hop(over, 1, 0)
        attend_grad, output_grad, *small_grads = call(
            finish_body,
            (shape(ROWS, 3 * D, dtype=F32), shape(ROWS, D, dtype=F32))
            + tuple(shape(n, ROWS, dtype=F32) for n in (8, 4, 2, 1, 1)),
            [SMEM] + [VM] * 4,
            [pltpu.VMEM((128, 128), F32)],
            ties=(result,),
        )(pos, own, over, got, got_over)
        in_grad, out_grad = call(
            place_second_body,
            (shape(ROWS, E_FFN, 2 * FF, dtype=F32), shape(FF // GROUP, E_FFN, D, dtype=F32)),
            [SMEM] + [VM] * 4 + [ANY] * 2,
            place_scratch,
            where=pl.ANY,
            aliases={5: 0, 6: 1},
        )(pos, *blocks_1, *placed)

        if spread > 1:
            attend_grad, output_grad, in_grad, out_grad = (
                lax.psum_scatter(
                    v, "shard", scatter_dimension=0, axis_index_groups=lows, tiled=True
                )
                for v in (attend_grad, output_grad, in_grad, out_grad)
            )
            small_grads = [
                lax.psum_scatter(
                    v, "shard", scatter_dimension=1, axis_index_groups=lows, tiled=True
                )
                for v in small_grads
            ]
        return (
            result,
            stream_grad,
            logits_grad.T,
            small_grads[3][0],
            attend_grad,
            output_grad,
            small_grads[4][0],
            small_grads[0].T,
            small_grads[1].T,
            small_grads[2].T,
            in_grad,
            out_grad,
        )

    return local


def solution(mesh):
    tokens = P(("rep", "shard"), None)
    weight = (P("shard"), P("shard", None), P("shard", None, None))
    return jax.shard_map(
        plan(mesh),
        mesh=mesh,
        in_specs=(tokens,) * 6
        + (weight[0], weight[1], weight[1], weight[0])
        + (weight[1],) * 3
        + (weight[2],) * 2,
        out_specs=(tokens,) * 3
        + (weight[0], weight[1], weight[1], weight[0])
        + (weight[1],) * 3
        + (weight[2],) * 2,
        check_vma=False,
    )
```

```python
import math

import jax
import jax.numpy as jnp
import numpy as np
from jax import lax
from jax.experimental import pallas as pl
from jax.experimental.pallas import tpu as pltpu
from jax.sharding import PartitionSpec as P

H = 12
HD = 64
FF = 2048
E_FFN = 4
NC = 2
NE = 8
CAP = 64
D = 768
T = 256
GROUP = 8
ROWS = D // GROUP
HALF = ROWS // 2
WIDE = 2 * D
EXTRA = 128
PACK = 576
QUARTER = FF // 4

EPSILON = 1e-06
BF = jnp.bfloat16
F32 = jnp.float32
I32 = jnp.int32
AXES = ("rep", "shard")
VMEM_LIMIT = 46 << 20


def nn(a, b):
    return lax.dot_general(a, b, (((1,), (0,)), ((), ())), preferred_element_type=F32)


def nt(a, b):
    return lax.dot_general(a, b, (((1,), (1,)), ((), ())), preferred_element_type=F32)


def tn(a, b):
    return lax.dot_general(a, b, (((0,), (0,)), ((), ())), preferred_element_type=F32)


def exact(a, b, dims):
    return lax.dot_general(
        a, b, (dims, ((), ())), precision=lax.Precision.HIGHEST, preferred_element_type=F32
    )


def iota(shape, dim):
    return lax.broadcasted_iota(I32, shape, dim)


def split(v):
    high = v.astype(BF)
    return high, (v - high.astype(F32)).astype(BF)


def tables():
    half = HD // 2
    position = np.arange(T, dtype=np.float32)
    frequency = np.exp(
        np.arange(half, dtype=np.float32) * np.float32(-2.0 * math.log(10000.0) / HD)
    ).astype(np.float32)
    angle = (position[:, None] * frequency[None, :]).astype(np.float32)
    cosine, sine = np.cos(angle), np.sin(angle)
    return (
        np.concatenate([cosine] * 4, axis=1).astype(np.float32),
        np.concatenate([-sine, sine] * 2, axis=1).astype(np.float32),
    )


def swapped(tile):
    lane = iota(tile.shape, 1) % HD
    return jnp.where(lane < HD // 2, pltpu.roll(tile, 96, 1), pltpu.roll(tile, 32, 1))


def call(body, out_shape, in_specs, scratch=(), where=pltpu.VMEM, aliases={}, ties=()):
    count = len(in_specs)

    def run(*args):
        return pl.pallas_call(
            lambda *refs: body(*refs[:count], *refs[count + len(ties) :]),
            out_shape=out_shape,
            in_specs=in_specs + [pl.BlockSpec(memory_space=pl.ANY)] * len(ties),
            out_specs=where if isinstance(where, tuple) else jax.tree.map(
                lambda v: pl.BlockSpec(memory_space=pltpu.SMEM if v.shape == (1,) else where),
                out_shape,
            ),
            scratch_shapes=list(scratch),
            input_output_aliases=aliases,
            compiler_params=pltpu.CompilerParams(vmem_limit_bytes=VMEM_LIMIT),
            cost_estimate=pl.CostEstimate(flops=0, bytes_accessed=0, transcendentals=0),
        )(*args, *ties)

    return run


def gate(values, others):
    count = len(values)
    return pl.pallas_call(
        lambda *refs: None,
        out_shape=[jax.ShapeDtypeStruct(v.shape, v.dtype) for v in values],
        in_specs=[pl.BlockSpec(memory_space=pl.ANY)] * (count + len(others)),
        out_specs=[pl.BlockSpec(memory_space=pl.ANY)] * count,
        input_output_aliases={n: n for n in range(count)},
    )(*values, *others)


SMEM = pl.BlockSpec(memory_space=pltpu.SMEM)
VM = pl.BlockSpec(memory_space=pltpu.VMEM)
ANY = pl.BlockSpec(memory_space=pl.ANY)


def shape(*dims, dtype=BF):
    return jax.ShapeDtypeStruct(dims, dtype)


def start_weights(pos, pieces, target, sems, extra=False):
    x, c, z, y = (pos[i] for i in range(4))
    copies = []
    for p in range(4):
        column = pl.multiple_of((x ^ (p >> 1)) * WIDE, 128)
        for cr in range(2):
            for kz in range(4):
                row = ((z ^ kz) * 2 + (y ^ (p & 1))) * ROWS + (c ^ cr) * HALF
                rows = pl.ds(pl.multiple_of(row, 16), HALF)
                piece = pieces[2 * p + cr].at[pl.ds(kz * HALF, HALF)]
                copies.append(
                    pltpu.make_async_copy(
                        piece.at[:, pl.ds(0, WIDE)],
                        target.at[rows, pl.ds(column, WIDE)],
                        sems.at[len(copies)],
                    )
                )
                if extra and p < 2:
                    copies.append(
                        pltpu.make_async_copy(
                            piece.at[:, pl.ds(WIDE, EXTRA)],
                            target.at[rows, pl.ds(2 * WIDE, EXTRA)],
                            sems.at[len(copies)],
                        )
                    )
    for copy in copies:
        copy.start()
    return copies


def group_body(pos, attend, output, router, mix, vector, gain1, gain2, out, small):
    x, c = pos[0], pos[1]
    rows = pl.ds(pl.multiple_of(c * HALF, 16), HALF)
    unit = jnp.where(iota((16, 128), 0) == iota((16, 128), 1), 1.0, 0.0).astype(BF)
    small[0:8, :], small[8:12, :], small[12:14, :] = router[...], mix[...], vector[...]
    small[14:15, :], small[15:16, :] = gain1[...], gain2[...]
    extra = tn(small[...], unit)
    out[:, WIDE:] = jnp.where(c == 0, extra[0:HALF], extra[HALF:]).astype(BF)

    @pl.when(x == 0)
    def _():
        out[:, :WIDE] = attend[rows, 0:WIDE]

    @pl.when(x == 1)
    def _():
        out[:, :D] = attend[rows, WIDE:]
        out[:, D:WIDE] = output[rows, :]


def expert_at_body(pos, out):
    out[0] = 2 * pos[0] + pos[3]


def cut_across_body(pos, ein, eout, out):
    cut_body(pos, ein, eout, out.at[pl.ds(0, PACK)], out.at[pl.ds(PACK, PACK)])


def cut_body(pos, ein, eout, near, far):
    c, z = pos[1], pos[2]
    lane = iota((ROWS, 128), 1)
    for zr in range(2):
        low, target, base = (z & 1) ^ zr, (near, far)[zr], 0
        for half in range(2):
            for t in range(4):
                a, b = (
                    ein[:, pl.ds(pl.multiple_of((half * 16 + 4 * t + 2 * o + low) * 128, 128), 128)]
                    .astype(F32) for o in range(2)
                )
                first = jnp.where(c == 0, a, pltpu.roll(a, 64, 1))
                second = jnp.where(c == 0, pltpu.roll(b, 64, 1), b)
                m, cols = 2 * half + t // 2, slice((t % 2) * 128, (t % 2 + 1) * 128)
                target[base + m * ROWS : base + (m + 1) * ROWS, cols] = jnp.where(
                    lane < 64, first, second
                ).astype(BF)
        row = pl.multiple_of((2 * low + c) * 64, 64)
        for n in range(3):
            at = base + 4 * ROWS + n * 64
            target[at : at + 64, :] = eout[pl.ds(row, 64), n * 256 : (n + 1) * 256]

def apart(pair, scale=1.0):
    first = iota(pair.shape, 1) < HD
    value = pair.astype(F32) * scale
    return jnp.concatenate(
        [jnp.where(first, value, 0.0), jnp.where(first, 0.0, value)], axis=0
    ).astype(BF)


def attend_body(
    pos, stream, seg, cos, sin, disp, w0, w1, w2, w3, w4, w5, w6, w7,
    normed_any, q_any, k_any, v_any, probs_any, mixed_any, hidden_any, routed_out, small_out, output_any,
    x0, x1, x2, x3, weights, sems, normed_out, q_out, k_out, v_out, probs_out, mixed_out, hidden_out, out_sems,
):
    copies = start_weights(pos, (w0, w1, w2, w3, w4, w5, w6, w7), weights, sems, extra=True)
    s = stream[...]
    r1 = lax.rsqrt(jnp.mean(s * s, axis=1, keepdims=True) + EPSILON)
    row, col = iota((T, T), 0), iota((T, T), 1)
    segf = seg[...].astype(F32)
    segcol = jnp.sum(jnp.where(row == col, segf, 0.0), axis=1, keepdims=True)
    allowed = (segcol == segf) & (col <= row)
    cosine, sine = cos[...], sin[...]
    for copy in copies:
        copy.wait()
    small = jnp.transpose(weights[:, 2 * WIDE :].astype(F32))[0:16]
    small_out[...] = small.astype(BF)
    normed = (s * r1 * small[14:15, :]).astype(BF)
    normed_out[...] = normed
    leaving = []

    def leave(source, target):
        leaving.append(pltpu.make_async_copy(source, target, out_sems.at[len(leaving)]))
        leaving[-1].start()

    leave(weights.at[:, pl.ds(3 * D, D)], output_any)
    leave(normed_out, normed_any)
    for n in range(9):
        part = nn(normed, weights[:, n * 256 : (n + 1) * 256])
        out, base = (q_out, k_out, v_out)[n // 3], (n % 3) * 256
        for t in range(2):
            tile = part[:, t * 128 : (t + 1) * 128]
            if n < 6:
                tile = tile * cosine + swapped(tile) * sine
            out[:, base + t * 128 : base + (t + 1) * 128] = tile.astype(BF)
    for source, target in ((q_out, q_any), (k_out, k_any), (v_out, v_any)):
        leave(source, target)
    first = iota((T, 128), 1) < HD
    for j in range(H // 2):
        cols = slice(j * 128, (j + 1) * 128)
        q2, k2, v2 = q_out[:, cols], k_out[:, cols], v_out[:, cols]
        halves = []
        for hh in range(2):
            mask = first if hh == 0 else ~first
            qm = jnp.where(mask, q2.astype(F32) * (1.0 / math.sqrt(HD)), 0.0).astype(BF)
            scores = jnp.where(allowed, nt(qm, k2), -1e30)
            raised = jnp.exp(scores - jnp.max(scores, axis=1, keepdims=True))
            probs = (raised * (1.0 / jnp.sum(raised, axis=1, keepdims=True))).astype(BF)
            probs_out[2 * j + hh] = probs
            halves.append(nn(probs, v2))
        mixed_out[:, cols] = jnp.where(first, halves[0], halves[1]).astype(BF)
        leave(probs_out.at[pl.ds(2 * j, 2)], probs_any.at[pl.ds(2 * j, 2)])
    leave(mixed_out, mixed_any)
    output = weights[:, 3 * D : 4 * D]
    hidden = s + nn(mixed_out[...], output)
    hidden_out[...] = hidden
    leave(hidden_out, hidden_any)
    r2 = lax.rsqrt(jnp.mean(hidden * hidden, axis=1, keepdims=True) + EPSILON)
    routed = (hidden * r2 * small[15:16, :]).astype(BF)
    routed_out[...] = routed
    slots = tn(disp[...], routed).astype(BF)
    for p, out in enumerate((x0, x1, x2, x3)):
        out[...] = slots[p * CAP : (p + 1) * CAP]
    for copy in leaving:
        copy.wait()


def route_body(pos, routes, order, grad, prev, g0, g1, g2, g3, disp_out, meta_out, flipped):
    here = 2 * pos[0] + pos[3]
    row, col = iota((T, T), 0), iota((T, T), 1)
    lane = iota((T, 128), 1)
    flipped[...] = jnp.zeros((128, T), F32)
    flipped[0:NE, :] = prev[...]
    flipped[NE : NE + 2, :] = routes[...].astype(F32)
    meta = jnp.transpose(flipped[...])
    meta_out[...] = meta
    lanef = lane.astype(F32)
    first, second = meta[:, NE : NE + 1], meta[:, NE + 1 : NE + 2]
    chosen = ((first == lanef) | (second == lanef)) & (lane < E_FFN)
    claims = jnp.where(order[...] == row, 1.0, 0.0).astype(BF)
    ranked = tn(claims, jnp.where(chosen, 1.0, 0.0).astype(BF))
    before = nn(jnp.where(col < row, 1.0, 0.0).astype(BF), ranked.astype(BF))
    place = nn(claims, before.astype(BF))
    kept = chosen & (place < CAP)
    dispatch = jnp.zeros((T, T), F32)
    colf = col.astype(F32)
    for p in range(4):
        mine = kept & (lane == (here ^ p))
        target = jnp.sum(jnp.where(mine, place + (p * CAP + 1.0), 0.0), axis=1, keepdims=True)
        dispatch = dispatch + jnp.where(colf == target - 1.0, 1.0, 0.0)
    dispatch = dispatch.astype(BF)
    disp_out[...] = dispatch
    slots = tn(dispatch, grad[...].astype(BF)).astype(BF)
    high, low = split(jnp.where(lane < NE, meta, 0.0))
    extra = tn(dispatch, high), pltpu.roll(tn(dispatch, low), 16, 1)
    extra = (extra[0] + extra[1]).astype(BF)
    for p, out in enumerate((g0, g1, g2, g3)):
        out[:, :D] = slots[p * CAP : (p + 1) * CAP]
        out[:, D:] = extra[p * CAP : (p + 1) * CAP]


def column(v, lane, index):
    return jnp.sum(jnp.where(lane == index, v, 0.0), axis=1, keepdims=True)


def chance(logits, lane):
    masked = jnp.where(lane < NE, logits, -1e30)
    raised = jnp.where(lane < NE, jnp.exp(masked - jnp.max(masked, axis=1, keepdims=True)), 0.0)
    return raised / jnp.sum(raised, axis=1, keepdims=True)


def router_body(hidden, routed, small, meta, grad, base_out, aux_out):
    lane = iota((T, 16), 1)
    rin = routed[...].astype(F32)
    g = grad[...]
    logits = nt(routed[...], small[...])
    chances = chance(logits + jnp.where(lane < NE, meta[:, 0:16], 0.0), lane)
    lanef = lane.astype(F32)
    chosen = (meta[:, NE : NE + 1] == lanef) | (meta[:, NE + 1 : NE + 2] == lanef)
    combine = jnp.where(chosen, chances, 0.0)
    copy_weight = column(combine, lane, E_FFN + 1)
    copy_grad = jnp.sum(g * rin, axis=1, keepdims=True)
    base = hidden[...] + copy_weight * rin
    others = jnp.where(lane == E_FFN + 1, copy_grad, 0.0)
    mixing_grad = jnp.zeros((T, 16), F32)
    factor = copy_weight
    for n in range(NC):
        l0, l1 = column(logits, lane, 8 + 2 * n), column(logits, lane, 9 + 2 * n)
        a0, a1 = 1.0 / (1.0 + jnp.exp(l1 - l0)), 1.0 / (1.0 + jnp.exp(l0 - l1))
        vector = small[12 + n : 13 + n, :].astype(F32)
        weight = column(combine, lane, E_FFN + 2 + n)
        base = base + weight * (a0 * rin + a1 * vector)
        vector_dot = jnp.sum(g * vector, axis=1, keepdims=True)
        others = others + jnp.where(
            lane == E_FFN + 2 + n, a0 * copy_grad + a1 * vector_dot, 0.0
        )
        d0, d1 = weight * copy_grad, weight * vector_dot
        total = a0 * d0 + a1 * d1
        mixing_grad = mixing_grad + jnp.where(lane == 8 + 2 * n, a0 * (d0 - total), 0.0)
        mixing_grad = mixing_grad + jnp.where(lane == 9 + 2 * n, a1 * (d1 - total), 0.0)
        mixing_grad = mixing_grad + jnp.where(lane == 12 + n, a1 * weight, 0.0)
        factor = factor + a0 * weight
    base_out[...] = base
    aux_out[:, 0:16] = chances
    aux_out[:, 16:32] = combine
    aux_out[:, 32:48] = jnp.where(chosen, others, 0.0)
    aux_out[:, 48:64] = mixing_grad
    aux_out[:, 64:128] = jnp.broadcast_to(factor, (T, 64))


def expert_body(
    pos, x0, x1, x2, x3, g0, g1, g2, v0, v1, v2, v3, v4, v5, v6,
    send_out, keep_out, act_any, grad_any, wout_out, win_out, act_out, grad_out, sems,
):
    z, y = pos[2], pos[3]
    near, far = pl.ds(0, PACK), pl.ds(PACK, PACK)
    pieces = (v0, v1, v2.at[near], v2.at[far], v3, v4, v5, v6)
    for n, piece in enumerate(pieces):
        shard = (z ^ (n // 2)) * 2 + (y ^ (n % 2))
        row = pl.multiple_of(shard * ROWS, 16)
        for m in range(4):
            win_out[pl.ds(row, ROWS), m * 256 : (m + 1) * 256] = piece[m * ROWS : (m + 1) * ROWS, :]
        row = pl.multiple_of(shard * 64, 64)
        for m in range(3):
            wout_out[pl.ds(row, 64), m * 256 : (m + 1) * 256] = piece[
                4 * ROWS + m * 64 : 4 * ROWS + (m + 1) * 64, :
            ]
    win, wout = win_out[...], wout_out[...]
    diagonal = iota((256, 256), 0) == iota((256, 256), 1)
    copies = []
    grads = (g0[:, :D], g1[:, :D], g2[0:256, :D], g2[256:512, :D])
    for b, (xs, gs) in enumerate(zip((x0, x1, x2, x3), grads)):
        rows = slice(b * 256, (b + 1) * 256)
        gate_up = nn(xs[...], win)
        a, u = gate_up[:, :QUARTER], gate_up[:, QUARTER:]
        sigma = 1.0 / (1.0 + jnp.exp(-a))
        swish = a * sigma
        activated = (swish * u).astype(BF)
        act_out[rows, :] = activated
        back = nt(gs, wout)
        dots = jnp.sum(activated.astype(F32) * back, axis=1, keepdims=True)
        dots = jnp.sum(jnp.where(diagonal, dots, 0.0), axis=0, keepdims=True)
        gate_grad = back * u * sigma * (1.0 + a * (1.0 - sigma))
        both = jnp.concatenate([gate_grad.astype(BF), (back * swish).astype(BF)], axis=1)
        grad_out[rows, :] = both
        slot_grad = nt(both, win)
        for source, target in ((act_out, act_any), (grad_out, grad_any)):
            part = pl.ds(b * 256, 256)
            copies.append(
                pltpu.make_async_copy(source.at[part], target.at[part], sems.at[len(copies)])
            )
            copies[-1].start()
        at, out = (b % 2) * 272, (keep_out, send_out)[b // 2]
        out[at : at + 256, :] = slot_grad.astype(BF)
        out[at + 256 : at + 272, :] = jnp.zeros((16, D), BF)
        out[at + 256 : at + 258, 0:256] = jnp.concatenate(split(dots), axis=0)
    for copy in copies:
        copy.wait()


def dots_of(ref, at):
    return ref[at : at + 1, 0:256].astype(F32) + ref[at + 1 : at + 2, 0:256].astype(F32)


def fold_body(keep, got, send_out, keep_out):
    for n, out in ((1, send_out), (0, keep_out)):
        at = n * 272
        total = keep[at : at + 256, :].astype(F32) + got[at : at + 256, :].astype(F32)
        dots = dots_of(keep, at + 256) + dots_of(got, at + 256)
        out[0:256, :] = total.astype(BF)
        out[256:272, :] = jnp.zeros((16, D), BF)
        out[256:258, 0:256] = jnp.concatenate(split(dots), axis=0)


def spread_body(keep, got, r0, r1, r2, r3):
    total = (keep[0:256, :].astype(F32) + got[0:256, :].astype(F32)).astype(BF)
    high, low = split(dots_of(keep, 256) + dots_of(got, 256))
    for p, out in enumerate((r0, r1, r2, r3)):
        out[0:CAP, :] = total[p * CAP : (p + 1) * CAP]
        out[CAP : CAP + 16, :] = jnp.zeros((16, D), BF)
        out[CAP : CAP + 2, 0:256] = jnp.concatenate([high, low], axis=0)


def slots_out_body(act, wout, send_out, keep_out):
    for b in range(4):
        part = nn(act[b * 256 : (b + 1) * 256, :], wout[...]).astype(BF)
        out = (keep_out, send_out)[b // 2]
        out[(b % 2) * 256 : (b % 2 + 1) * 256, :] = part


def weight_grad_body(
    pos, x0, x1, x2, x3, g0, g1, g2, act, grad, small,
    d0, d1, d2, d3, scaled, whole, rows_out,
):
    x, z, y = pos[0], pos[2], pos[3]
    lane = iota((256, 16), 1)
    expert = 2 * x + y
    total = jnp.zeros((QUARTER, D), F32)
    xs = jnp.concatenate([v[...] for v in (x0, x1, x2, x3)], axis=0)
    grads = (g0[...], g1[...], g2[0:256, :], g2[256:512, :])
    for b, (xv, gs) in enumerate(zip((x0, x1, x2, x3), grads)):
        rows = slice(b * 256, (b + 1) * 256)
        prev = gs[:, D : D + 16].astype(F32) + gs[:, D + 16 : D + 32].astype(F32)
        chances = chance(nt(xv[...], small[...]) + jnp.where(lane < NE, prev, 0.0), lane)
        weight = column(chances, lane, expert)
        scaled[rows, :] = (grad[rows, :].astype(F32) * weight).astype(BF)
        total = total + tn(act[rows, :], (gs[:, :D].astype(F32) * weight).astype(BF))
    rows_out[...] = total.astype(BF)
    for n in range(4):
        cols = slice(n * 256, (n + 1) * 256)
        whole[:, cols] = tn(xs, scaled[:, cols]).astype(BF)
    for n in range(8):
        out, base = (d0, d1, d2, d3)[n // 2], (n % 2) * PACK
        shard = (z ^ (n // 2)) * 2 + (y ^ (n % 2))
        row = pl.multiple_of(shard * ROWS, 16)
        for m in range(4):
            out[base + m * ROWS : base + (m + 1) * ROWS, :] = whole[
                pl.ds(row, ROWS), m * 256 : (m + 1) * 256
            ]
        row, base = pl.multiple_of(shard * 64, 64), base + 4 * ROWS
        for m in range(3):
            out[base + m * 64 : base + (m + 1) * 64, :] = rows_out[
                pl.ds(row, 64), m * 256 : (m + 1) * 256
            ]


def back_body(
    pos, r0, r1, r2, r3, disp, hidden_in, routed, aux, grad, small, q_any, k_any, v_any,
    probs_any, cos, sin, output,
    hidden_any, logits_out, small_out, pq, pk, pv, pa, q, k, v, probs, hidden_out, sems,
):
    x, c, z, y = (pos[i] for i in range(4))
    coming = [
        pltpu.make_async_copy(source, target, sems.at[n])
        for n, (source, target) in enumerate(((q_any, q), (k_any, k), (v_any, v), (probs_any, probs)))
    ]
    for copy in coming:
        copy.start()
    here = 2 * x + y
    lane = iota((T, 16), 1)
    block = iota((T, T), 1) // CAP
    block_row = iota((1, T), 1) // CAP
    dispf = disp[...].astype(F32)
    g, hidden, rin = grad[...], hidden_in[...], routed[...].astype(F32)
    chances, combine = aux[:, 0:16], aux[:, 16:32]
    dots = jnp.zeros((1, T), F32)
    weight = jnp.zeros((T, T), F32)
    chance_grad = aux[:, 32:48]
    for p, r in enumerate((r0, r1, r2, r3)):
        part = r[CAP : CAP + 1, 0:T].astype(F32) + r[CAP + 1 : CAP + 2, 0:T].astype(F32)
        dots = jnp.where(block_row == p, part, dots)
        weight = jnp.where(block == p, column(combine, lane, here ^ p), weight)
    picked = dispf * dots
    for p in range(4):
        each = jnp.sum(jnp.where(block == p, picked, 0.0), axis=1, keepdims=True)
        chance_grad = chance_grad + jnp.where(lane == (here ^ p), each, 0.0)
    logit_grad = chances * (chance_grad - jnp.sum(chances * chance_grad, axis=1, keepdims=True))
    logits_out[...] = jnp.transpose(logit_grad)[0:NE]
    extra = aux[:, 48:64]
    mix_grad = jnp.where((lane >= 8) & (lane < 12), extra, 0.0)
    all_grad = logit_grad + mix_grad
    pair = jnp.concatenate(split(all_grad), axis=1)
    returned = jnp.concatenate([r[0:CAP, :] for r in (r0, r1, r2, r3)], axis=0)
    high, low = split(dispf * weight)
    smallf = small[...].astype(F32)
    routed_grad = (
        aux[:, 64:65] * g + nn(high, returned) + nn(low, returned)
        + nn(pair, jnp.concatenate([small[...], small[...]], axis=0))
    )
    r2n = lax.rsqrt(jnp.mean(hidden * hidden, axis=1, keepdims=True) + EPSILON)
    scaled = routed_grad * smallf[15:16, :]
    hidden_grad = (
        g + r2n * scaled
        - hidden * (r2n * r2n * r2n) * jnp.mean(scaled * hidden, axis=1, keepdims=True)
    )
    attn_grad = hidden_grad.astype(BF)
    hidden_out[...] = hidden_grad
    leaving = pltpu.make_async_copy(hidden_out, hidden_any, sems.at[4])
    leaving.start()
    both = tn(pair, routed[...])
    small_out[...] = both[0:16] + both[16:32]
    pair = jnp.concatenate(split(jnp.where(lane >= 12, extra, 0.0)), axis=1)
    g_high, g_low = split(g)
    both = tn(pair, g_high) + tn(pair, g_low)
    small_out[12:14, :] = both[12:14] + both[28:30]
    small_out[15:16, :] = jnp.sum(routed_grad * hidden * r2n, axis=0, keepdims=True)
    mixed_grad = nt(attn_grad, output[...]).astype(BF)
    pa[...] = attn_grad
    for copy in coming:
        copy.wait()
    first = iota((T, 128), 1) < HD
    cosine, sine = cos[...], sin[...]
    scale = 1.0 / math.sqrt(HD)
    for j in range(H // 2):
        cols = slice(j * 128, (j + 1) * 128)
        q2, k2, v2, do2 = q[:, cols], k[:, cols], v[:, cols], mixed_grad[:, cols]
        do, pb = apart(do2), jnp.concatenate([probs[2 * j], probs[2 * j + 1]], axis=0)
        pf = pb.astype(F32)
        prob_grad = nt(do, v2)
        inner = jnp.sum(pf * prob_grad, axis=1, keepdims=True)
        score_grad = (pf * (prob_grad - inner)).astype(BF)
        both = nn(score_grad, k2)
        dq, dk, dv = jnp.where(first, both[0:T], both[T:]), tn(score_grad, apart(q2)), tn(pb, do)
        dq, dk = dq * scale, dk * scale
        pq[:, cols] = (dq * cosine - swapped(dq) * sine).astype(BF)
        pk[:, cols] = (dk * cosine - swapped(dk) * sine).astype(BF)
        pv[:, cols] = dv.astype(BF)
    leaving.wait()


def turn_body(pos, n0, n1, m0, m1, a_out, b_out, flipped):
    c, z, y = pos[1], pos[2], pos[3]
    for out, parts in ((a_out, (n0, n1)), (b_out, (m0, m1))):
        for n, part in enumerate(parts):
            flipped[...] = jnp.transpose(part[...].astype(F32)).astype(BF)
            for yr in range(2):
                for kz in range(4):
                    row = ((z ^ kz) * 2 + (y ^ yr)) * ROWS + c * HALF
                    at = (4 * yr + kz) * HALF
                    out[at : at + HALF, n * T : (n + 1) * T] = flipped[
                        pl.ds(pl.multiple_of(row, 16), HALF), :
                    ]


def weight_body(
    pos, normed, mixed, q0, k0, v0, a0, q1, k1, v1, a1, small0, small1,
    o0, o1, o2, o3, extra, both, turned,
):
    x, c, z, y = (pos[i] for i in range(4))
    extra[...] = jnp.zeros((EXTRA, D), F32)
    extra[0:16, :] = small0[...] + small1[...]
    small = jnp.transpose(extra[...]).astype(BF)
    for n, (own, other) in enumerate(((q0, q1), (k0, k1), (v0, v1), (a0, a1))):
        cols = slice(n * D, (n + 1) * D)
        both[0:T, cols], both[T:, cols] = own[...], other[...]
    for p, out in enumerate((o0, o1, o2, o3)):
        side = x ^ (p >> 1)
        rows = slice((p & 1) * 4 * HALF, ((p & 1) + 1) * 4 * HALF)
        left = normed[rows, :]
        right = jnp.where(side == 1, mixed[rows, :], left)
        at = pl.multiple_of(side * WIDE, 128)
        out[:, 0:D] = nn(left, both[:, pl.ds(at, D)]).astype(BF)
        out[:, D:WIDE] = nn(right, both[:, pl.ds(pl.multiple_of(at + D, 128), D)]).astype(BF)
    turned[...] = small
    for p, out in enumerate((o0, o1, o2, o3)):
        for kz in range(4):
            row = ((z ^ kz) * 2 + (y ^ (p & 1))) * ROWS + c * HALF
            value = turned[pl.ds(pl.multiple_of(row, 16), HALF), :]
            out[kz * HALF : (kz + 1) * HALF, WIDE:] = jnp.where(
                x ^ (p >> 1) == 0, value, jnp.zeros_like(value)
            )


def stream_body(
    pos, pq, pk, pv, stream, hidden_grad, small, w0, w1, w2, w3, w4, w5, w6, w7, out, weights, sems
):
    copies = start_weights(pos, (w0, w1, w2, w3, w4, w5, w6, w7), weights, sems)
    s = stream[...]
    r1 = lax.rsqrt(jnp.mean(s * s, axis=1, keepdims=True) + EPSILON)
    for copy in copies:
        copy.wait()
    scaled = nt(pq[...], weights[:, :D]) + nt(pk[...], weights[:, D : 2 * D])
    scaled = scaled + nt(pv[...], weights[:, 2 * D : 3 * D])
    scaled = scaled * small[14:15, :].astype(F32)
    out[...] = (
        hidden_grad[...] + r1 * scaled
        - s * (r1 * r1 * r1) * jnp.mean(scaled * s, axis=1, keepdims=True)
    )


def result_body(pos, base, disp, aux, r0, r1, r2, r3, out):
    here = 2 * pos[0] + pos[3]
    lane = iota((T, 16), 1)
    block = iota((T, T), 1) // CAP
    combine = aux[:, 16:32]
    weight = jnp.zeros((T, T), F32)
    for p in range(4):
        weight = jnp.where(block == p, column(combine, lane, here ^ p), weight)
    high, low = split(disp[...].astype(F32) * weight)
    returned = jnp.concatenate([r[...] for r in (r0, r1, r2, r3)], axis=0)
    out[...] = (base[...] + nn(high, returned) + nn(low, returned)).astype(BF)


def finish_body(
    pos, own, over, got, got_over, attend, gain1,
    attend_out, output_out, router_out, mix_out, vector_out, gain1_out, gain2_out, extra,
):
    x, c = pos[0], pos[1]
    for cr, (near, far) in enumerate(((own, over), (got, got_over))):
        rows = pl.ds(pl.multiple_of((c ^ cr) * HALF, 16), HALF)
        a, b = near[...].astype(F32), far[...].astype(F32)
        first, second = jnp.where(x == 0, a, b), jnp.where(x == 0, b, a)
        attend_out[rows, 0:WIDE] = first[:, :WIDE]
        attend_out[rows, WIDE:] = second[:, :D]
        output_out[rows, :] = second[:, D:WIDE]
        extra[rows, :] = first[:, WIDE:]
    extra[ROWS:, :] = jnp.zeros((128 - ROWS, 128), F32)
    small = jnp.transpose(extra[...])[0:16, 0:ROWS]
    router_out[...], mix_out[...], vector_out[...] = small[0:8], small[8:12], small[12:14]
    gain2_out[...] = small[15:16]
    along = jnp.sum(attend_out[...] * attend[...].astype(F32), axis=1, keepdims=True)
    row, col = iota((ROWS, ROWS), 0), iota((ROWS, ROWS), 1)
    along = jnp.sum(jnp.where(row == col, along, 0.0), axis=0, keepdims=True)
    gain1_out[...] = along / gain1[...].astype(F32)


def place_copies(pos, zr, blocks, in_out, out_out, ins, outs, sems, both):
    x, c, z, y = (pos[i] for i in range(4))
    here = 2 * x + y
    lane = iota((ROWS, 128), 1)
    low = (z & 1) ^ zr
    for cr in range(2):
        both[c ^ cr, : 2 * PACK, :] = blocks[2 * cr][...]
        both[c ^ cr, 2 * PACK :, :] = blocks[2 * cr + 1][...]
    copies = []
    for half in range(2):
        for s in range(8):
            m, cols = 2 * half + s // 4, slice((s % 4) // 2 * 128, ((s % 4) // 2 + 1) * 128)
            n = 8 * half + s
            for expert in range(E_FFN):
                rows = pl.ds(pl.multiple_of((expert ^ here) * PACK + m * ROWS, 16), ROWS)
                first, second = both[0, rows, cols].astype(F32), both[1, rows, cols].astype(F32)
                if s % 2:
                    first = pltpu.roll(first, HD, 1)
                else:
                    second = pltpu.roll(second, HD, 1)
                ins[n, :, expert, :] = jnp.where(lane < HD, first, second)
            tile = pl.multiple_of((half * 16 + 2 * s + low) * 128, 128)
            copies.append(
                pltpu.make_async_copy(ins.at[n], in_out.at[:, :, pl.ds(tile, 128)], sems.at[n])
            )
            copies[-1].start()
    for core in range(2):
        for expert in range(E_FFN):
            for n in range(3):
                rows = pl.ds(
                    pl.multiple_of((expert ^ here) * PACK + 4 * ROWS + n * 64, 16), 64
                )
                outs[core, :, expert, n * 256 : (n + 1) * 256] = both[core, rows, :].astype(F32)
        row = (2 * low + core) * 64
        copies.append(
            pltpu.make_async_copy(outs.at[core], out_out.at[pl.ds(row, 64)], sems.at[16 + core])
        )
        copies[-1].start()
    for copy in copies:
        copy.wait()


def place_first_body(pos, b0, b1, b2, b3, *rest):
    place_copies(pos, 0, (b0, b1, b2, b3), *rest)


def place_second_body(pos, b0, b1, b2, b3, in_old, out_old, *rest):
    place_copies(pos, 1, (b0, b1, b2, b3), *rest)


def plan(mesh):
    reps, shards = mesh.shape["rep"], mesh.shape["shard"]
    spread = shards // GROUP
    assert reps == E_FFN and shards % GROUP == 0
    lows = [[hi * spread + lo for lo in range(spread)] for hi in range(GROUP)]

    def flat(rep, hi, lo):
        return rep * shards + hi * spread + lo

    def hop(value, rmask, hmask):
        pairs = [
            (flat(r, h, w), flat(r ^ rmask, h ^ hmask, w))
            for r in range(reps) for h in range(GROUP) for w in range(spread)
        ]
        return lax.ppermute(value, AXES, pairs)

    XY = ((0, 0), (0, 1), (2, 0), (2, 1))

    def exchange(parts):
        return [parts[0]] + [hop(parts[p], *XY[p]) for p in (1, 2, 3)]

    def relay(parts):
        n = parts[0].shape[0]
        by_y = hop(jnp.concatenate([parts[1], parts[3]], axis=0), 0, 1)
        by_x = hop(jnp.concatenate([parts[2], by_y[n:]], axis=0), 2, 0)
        return [parts[0], by_y[:n], by_x[:n], by_x[n:]]

    def line(parts):
        return [parts[0]] + [hop(parts[kz], 0, 2 * kz) for kz in (1, 2, 3)]

    def after(value, *others):
        return gate([value], others)[0]

    def add(a, b):
        return (a.astype(F32) + b.astype(F32)).astype(BF)

    cos_table, sin_table = tables()
    place_scratch = [
        pltpu.VMEM((16, ROWS, E_FFN, 128), F32),
        pltpu.VMEM((2, 64, E_FFN, D), F32),
        pltpu.SemaphoreType.DMA((18,)),
        pltpu.VMEM((2, 4 * PACK, 256), BF),
    ]

    def local(
        stream, prev_logits, segments, routes, claim_order, out_cotangent,
        first_gain, attend_weight, output_weight, second_gain, router_weight,
        constant_mix, constant_vector, expert_in, expert_out,
    ):
        rep, shard = lax.axis_index("rep"), lax.axis_index("shard")
        high = shard // spread
        x, c, z, y = rep // 2, rep % 2, high // 2, high % 2
        pos = jnp.stack([x, c, z, y]).astype(I32)

        smalls = [router_weight.T, constant_mix.T, constant_vector.T, first_gain[None], second_gain[None]]
        if spread > 1:
            smalls = [
                lax.all_gather(v, "shard", axis_index_groups=lows, axis=1, tiled=True) for v in smalls
            ]
            attend_weight, output_weight, expert_in, expert_out = (
                lax.all_gather(v, "shard", axis_index_groups=lows, axis=0, tiled=True)
                for v in (attend_weight, output_weight, expert_in, expert_out)
            )

        def cut(at, body, out):
            ein = lax.dynamic_slice(expert_in, (0, at[0], 0), (ROWS, 1, 2 * FF))[:, 0]
            eout = lax.dynamic_slice(expert_out, (0, at[0], 0), (FF // GROUP, 1, D))[:, 0]
            return call(body, out, [SMEM] + [VM] * 2)(pos, ein, eout)

        mine = call(
            group_body,
            shape(HALF, WIDE + EXTRA),
            [SMEM] + [VM] * 7,
            [pltpu.VMEM((16, ROWS), BF)],
            ties=(),
        )(pos, attend_weight, output_weight, *smalls)
        w_lines = line([mine] * 4)
        w_column = jnp.concatenate(w_lines, axis=0)

        cut_across = cut([2 * x + (y ^ 1)], cut_across_body, shape(2 * PACK, 256))
        came = hop(cut_across, 0, 1)
        came = came[:PACK], came[PACK:]
        cut_own = cut([2 * x + y], cut_body, (shape(PACK, 256),) * 2)
        *g_parts, disp, meta = call(
            route_body,
            (shape(CAP, D + 128),) * 4 + (shape(T, T), shape(T, 128, dtype=F32)),
            [SMEM] + [VM] * 4,
            [pltpu.VMEM((128, T), F32)],
            ties=(mine,),
        )(pos, routes.T, claim_order, out_cotangent, prev_logits.T)

        g_first = jnp.concatenate(relay(g_parts), axis=0)

        w_column, = gate([w_column], [g_first])
        plane = [w_column] + [hop(w_column, *XY[p]) for p in (1, 2, 3)]
        pieces = [v for p in range(4) for v in (plane[p], hop(plane[p], 1, 0))]
        part_20 = hop(cut_own[0], 0, 4)
        part_30 = hop(gate([cut_own[1]], [part_20])[0], 0, 6)
        part_21 = hop(gate([came[0]], [part_20])[0], 0, 4)

        normed, q, k, v, probs, mixed, hidden, routed, small, output, *x_parts = call(
            attend_body,
            (shape(T, D),) * 4 + (shape(H, T, T), shape(T, D), shape(T, D, dtype=F32))
            + (shape(T, D), shape(16, D), shape(D, D)) + (shape(CAP, D),) * 4,
            [SMEM] + [VM] * 5 + [ANY] * 8,
            [pltpu.VMEM((D, 4 * D + EXTRA), BF), pltpu.SemaphoreType.DMA((48,))]
            + [pltpu.VMEM((T, D), BF)] * 4
            + [pltpu.VMEM((H, T, T), BF), pltpu.VMEM((T, D), BF), pltpu.VMEM((T, D), F32),
               pltpu.SemaphoreType.DMA((13,))],
            where=(ANY,) * 7 + (VM, VM, ANY) + (VM,) * 4,
            ties=(part_30, part_21, g_first),
        )(pos, stream, segments, cos_table, sin_table, disp, *pieces)
        normed_pair, mixed_pair = (normed, hop(normed, 1, 0)), (mixed, hop(mixed, 1, 0))
        turned = call(
            turn_body,
            (shape(D // 2, 2 * T),) * 2,
            [SMEM] + [VM] * 4,
            [pltpu.VMEM((D, T), BF)],
            ties=(),
        )(pos, *normed_pair, *mixed_pair)
        came_0, came_1 = came
        g_second = hop(g_first, 0, 2)

        part_31 = hop(came_1, 0, 6)
        part_1 = hop(gate([jnp.concatenate([cut_own[1], came[1]], axis=0)], [part_30])[0], 0, 2)
        x_first = jnp.concatenate(exchange(x_parts), axis=0)
        x_first, = gate([x_first], [part_31])
        x_second, x_third = hop(x_first, 0, 2), hop(x_first, 1, 0)
        g_other = hop(jnp.concatenate([g_first, g_second], axis=0), 1, 0)
        base, aux = call(
            router_body, (shape(T, D, dtype=F32), shape(T, 128, dtype=F32)), [VM] * 5
        )(hidden, routed, small, meta, out_cotangent)
        x_second, = gate([x_second], [aux, part_1, turned[0]])
        x_slots = (x_first, x_second, x_third, hop(x_second, 1, 0))
        g_slots = (g_first, g_second, g_other)
        expert_parts = (cut_own[0], came[0], part_1, part_20, part_21, part_30, part_31)

        send, keep, act, gate_up_grad, wout = call(
            expert_body,
            (shape(544, D), shape(544, D), shape(1024, QUARTER), shape(1024, 2 * QUARTER),
             shape(QUARTER, D)),
            [SMEM] + [VM] * 14,
            [pltpu.VMEM((D, 2 * QUARTER), BF), pltpu.VMEM((1024, QUARTER), BF),
             pltpu.VMEM((1024, 2 * QUARTER), BF), pltpu.SemaphoreType.DMA((8,))],
            where=(VM, VM, ANY, ANY, VM),
        )(pos, *x_slots, *g_slots, *expert_parts)
        got = hop(send, 1, 0)
        out_send, out_keep = call(slots_out_body, (shape(512, D),) * 2, [VM] * 2)(act, wout)
        send, keep = call(fold_body, (shape(272, D),) * 2, [VM] * 2, ties=(out_keep,))(keep, got)
        got, out_got = hop(send, 0, 2), hop(out_send, 1, 0)
        grad_parts = call(
            weight_grad_body,
            (shape(2 * PACK, 256),) * 4,
            [SMEM] + [VM] * 10,
            [pltpu.VMEM((1024, 2 * QUARTER), BF), pltpu.VMEM((D, 2 * QUARTER), BF),
             pltpu.VMEM((QUARTER, D), BF)],
            ties=(keep,),
        )(pos, *x_slots, *g_slots, act, gate_up_grad, small)
        back_parts = call(
            spread_body, (shape(CAP + 16, D),) * 4, [VM] * 2, ties=(grad_parts[0], out_got)
        )(keep, got)
        out_sum = add(out_keep, out_got)
        grad_2 = hop(gate([grad_parts[2]], [got])[0], 0, 4)
        out_half = hop(gate([out_sum[256:]], [back_parts[0]])[0], 0, 2)
        back_parts = exchange(back_parts)


        hidden_grad, logits_grad, small_grad, *projected = call(
            back_body,
            (shape(T, D, dtype=F32), shape(NE, T, dtype=F32), shape(16, D, dtype=F32))
            + (shape(T, D),) * 4,
            [SMEM] + [VM] * 10 + [ANY] * 4 + [VM] * 3,
            [pltpu.VMEM((T, D), BF)] * 3
            + [pltpu.VMEM((H, T, T), BF), pltpu.VMEM((T, D), F32), pltpu.SemaphoreType.DMA((5,))],
            where=(ANY,) + (VM,) * 6,
        )(pos, *back_parts, disp, hidden, routed, aux, out_cotangent, small,
          q, k, v, probs, cos_table, sin_table, output)

        w_sums = call(
            weight_body,
            (shape(4 * HALF, WIDE + EXTRA),) * 4,
            [SMEM] + [VM] * 12,
            [pltpu.VMEM((EXTRA, D), F32), pltpu.VMEM((2 * T, 4 * D), BF), pltpu.VMEM((D, EXTRA), BF)],
            ties=(grad_2,),
        )(pos, *turned, *projected, *(hop(v, 1, 0) for v in projected), small_grad, hop(small_grad, 1, 0))
        w_sums_near = w_sums[0]

        w_sums = exchange(w_sums)
        grad_1 = hop(gate([grad_parts[1]], [w_sums_near])[0], 0, 2)
        part_3, = gate([grad_parts[3]], [w_sums_near])
        grad_3 = hop(part_3, 0, 6)
        out_sum = add(out_sum[:256], out_half)
        w_total = add(add(w_sums[0], w_sums[1]), add(w_sums[2], w_sums[3]))

        def far_blocks(near, came):
            both = jnp.concatenate([near, came], axis=0)
            far = hop(both, 2, 0)
            return both, far, hop(both, 1, 0), hop(far, 1, 0)

        kept_0, = gate([grad_parts[0]], [w_sums_near])
        sum_0 = add(kept_0, grad_2)
        came_0 = hop(sum_0[PACK:], 0, 1)

        stream_grad = call(
            stream_body,
            shape(T, D, dtype=F32),
            [SMEM] + [VM] * 6 + [ANY] * 8,
            [pltpu.VMEM((D, 4 * D), BF), pltpu.SemaphoreType.DMA((32,))],
            ties=(came_0,),
        )(pos, *projected[:3], stream, hidden_grad, small, *pieces)
        blocks_0 = far_blocks(sum_0[:PACK], came_0)

        w_total, = gate([w_total], [grad_3, *blocks_0, stream_grad])
        w_lines = line([w_total[kz * HALF : (kz + 1) * HALF] for kz in range(4)])
        own = add(add(w_lines[0], w_lines[1]), add(w_lines[2], w_lines[3]))

        sum_1 = add(grad_1, grad_3)
        blocks_1 = far_blocks(sum_1[:PACK], hop(sum_1[PACK:], 0, 1))
        placed = call(
            place_first_body,
            (shape(ROWS, E_FFN, 2 * FF, dtype=F32), shape(FF // GROUP, E_FFN, D, dtype=F32)),
            [SMEM] + [VM] * 4,
            place_scratch,
            where=pl.ANY,
        )(pos, *blocks_0)
        in_grad, out_grad = call(
            place_second_body,
            (shape(ROWS, E_FFN, 2 * FF, dtype=F32), shape(FF // GROUP, E_FFN, D, dtype=F32)),
            [SMEM] + [VM] * 4 + [ANY] * 2,
            place_scratch,
            where=pl.ANY,
            aliases={5: 0, 6: 1},
        )(pos, *blocks_1, *placed)

        over, got = hop(own, 2, 0), hop(own, 1, 0)
        out_sum, = gate([out_sum], [w_total])
        outs = relay([out_sum[p * CAP : (p + 1) * CAP] for p in range(4)])
        result = call(result_body, shape(T, D), [SMEM] + [VM] * 7)(pos, base, disp, aux, *outs)
        over, = gate([over], [in_grad, result])
        got_over = hop(over, 1, 0)
        attend_grad, output_grad, *small_grads = call(
            finish_body,
            (shape(ROWS, 3 * D, dtype=F32), shape(ROWS, D, dtype=F32))
            + tuple(shape(n, ROWS, dtype=F32) for n in (8, 4, 2, 1, 1)),
            [SMEM] + [VM] * 6,
            [pltpu.VMEM((128, 128), F32)],
            ties=(result,),
        )(pos, own, over, got, got_over, attend_weight, smalls[3])

        if spread > 1:
            attend_grad, output_grad, in_grad, out_grad = (
                lax.psum_scatter(
                    v, "shard", scatter_dimension=0, axis_index_groups=lows, tiled=True
                )
                for v in (attend_grad, output_grad, in_grad, out_grad)
            )
            small_grads = [
                lax.psum_scatter(
                    v, "shard", scatter_dimension=1, axis_index_groups=lows, tiled=True
                )
                for v in small_grads
            ]
        return (
            result,
            stream_grad,
            logits_grad.T,
            small_grads[3][0],
            attend_grad,
            output_grad,
            small_grads[4][0],
            small_grads[0].T,
            small_grads[1].T,
            small_grads[2].T,
            in_grad,
            out_grad,
        )

    return local


def solution(mesh):
    tokens = P(("rep", "shard"), None)
    weight = (P("shard"), P("shard", None), P("shard", None, None))
    return jax.shard_map(
        plan(mesh),
        mesh=mesh,
        in_specs=(tokens,) * 6
        + (weight[0], weight[1], weight[1], weight[0])
        + (weight[1],) * 3
        + (weight[2],) * 2,
        out_specs=(tokens,) * 3
        + (weight[0], weight[1], weight[1], weight[0])
        + (weight[1],) * 3
        + (weight[2],) * 2,
        check_vma=False,
    )
```
